256 devices in a mesh: dp: 2 (over x_lo), ctx: 8 (over y, x_hi), exp: 16 (over z, core).
Axes of the slice: x: 4 (x_hi: 2, x_lo: 2; x = x_hi * 2 + x_lo), y: 4, z: 8, core: 2. Of those that a mesh axis runs over, the one named last changes fastest.
Arguments:
- queries: bfloat16 [32768, 4096], P(('dp', 'ctx', 'exp')), may hold values from -64 to 64
- keys: bfloat16 [32768, 256], P(('dp', 'ctx', 'exp')), may hold values from -24 to 24
- values: bfloat16 [32768, 256], P(('dp', 'ctx', 'exp')), may hold values from -6 to 6
- lengths: int32 [2, 12], P('dp'), may hold values from 1 to 2048, 16384 in all within a row
- hidden: bfloat16 [32768, 4096], P(('dp', 'ctx', 'exp')), may hold values from -6 to 6
- norm_gain: float32 [4096], replicated, may hold values from 0.1 to 1.9
- routes: int32 [32768, 2], P(('dp', 'ctx', 'exp')), may hold values from 0 to 15, all different within a row; in each aligned block of 128 rows (0 to 127, 128 to 255, ...) at most 24 rows name the same one
- gates: float32 [32768, 2], P(('dp', 'ctx', 'exp')), may hold values from 0.2 to 1
- w_gate: bfloat16 [16, 4096, 768], P('exp', None, ('dp', 'ctx')), may hold values from -0.09375 to 0.09375
- w_up: bfloat16 [16, 4096, 768], P('exp', None, ('dp', 'ctx')), may hold values from -0.09375 to 0.09375
- w_down: bfloat16 [16, 4096, 768], P('exp', None, ('dp', 'ctx')), may hold values from -0.21875 to 0.21875
Outputs:
- context: bfloat16 [32768, 4096], P(('dp', 'ctx', 'exp'))
- expert_mix: bfloat16 [32768, 4096], P(('dp', 'ctx', 'exp'))
The draws below stay inside these ranges and needn't reach their ends.
Inputs may be any that keep to these rules, and one draw needn't show every extreme that they name: `routes`: each row names 2 different experts. In the rows of one device (aligned blocks of 128 rows) no expert is named more than 24 times, a bound that some block reaches. `lengths`: each row sums to 16384; its longest rollout has exactly 2048 tokens.
All inputs are finite; a program needn't handle non-finite values.
Results may differ from the reference program's by a relative error of at most 0.014.
Values may be sent and summed in bfloat16 or wider, within the bound.
A program may use at most 192 MiB of HBM per device.

```python
import math
import jax
import jax.numpy as jnp
import numpy as np
from jax import lax

D = 4096
HEAD_WIDTH = 128
QUERY_HEADS = 32
KEY_HEADS = 2
FF = 768
TOPK = 2
ROLLOUTS = 12
DEVICE_TOKENS = 128
CONTEXT_TOKENS = 2048
REPLICA_TOKENS = 16384
TOKEN_COUNT = 32768
EXPERTS = 16
CAP = 24
N_DP = 2
N_CTX = 8
N_EXP = 16


def paired(key, lifting):
    query_key, key_random_seed, pick_key, power_key, nudge_key = jax.random.split(key, 5)
    head_grouping = QUERY_HEADS // KEY_HEADS
    initial_keys = jnp.clip(jax.random.normal(key_random_seed, (TOKEN_COUNT, KEY_HEADS, HEAD_WIDTH), jnp.float32), -5.0, 5.0)
    base_queries = jnp.clip(jax.random.normal(query_key, (TOKEN_COUNT, QUERY_HEADS, HEAD_WIDTH), jnp.float32), -5.0, 5.0)
    picked = (jax.random.randint(pick_key, (TOKEN_COUNT,), 0, 48) == 0).astype(jnp.float32) * lifting
    strength = jax.random.uniform(power_key, (TOKEN_COUNT, 1, 1), jnp.float32, 1.0, 3.0)
    lifted = initial_keys * (1.0 + 2.0 * picked[:, None, None])
    follow = jnp.roll(picked, -1)
    nudging = jax.random.uniform(nudge_key, (TOKEN_COUNT, 1, 1), jnp.float32, 0.002, 0.008)
    earlier = jnp.roll(lifted, -1, axis=0) * (1.0 - nudging)
    output_keys = jnp.where(follow[:, None, None] > 0, earlier, lifted)
    aligned = strength * jnp.repeat(lifted, head_grouping, axis=1)
    output_queries = jnp.where(picked[:, None, None] > 0, aligned, base_queries)
    return (output_queries.reshape(TOKEN_COUNT, QUERY_HEADS * HEAD_WIDTH), output_keys.reshape(TOKEN_COUNT, KEY_HEADS * HEAD_WIDTH))


def draw_queries(key, part):
    lifting = 0.0
    return paired(key, lifting)[0].astype(jnp.bfloat16)


def draw_keys(key, part):
    lifting = 0.0
    return paired(key, lifting)[1].astype(jnp.bfloat16)


def steps_of(key, dims, cuts, low, largest):
    gain, own = 1.0, jax.random.fold_in(key, 6)
    for position, blocks in cuts:
        draws = jnp.exp(jax.random.uniform(jax.random.fold_in(own, position), (blocks,), jnp.float32, low / len(cuts), largest / len(cuts)))
        gain = gain * jnp.repeat(draws, dims[position] // blocks).reshape([-1 if axis == position else 1 for axis in range(len(dims))])
    return gain


def length_profile(number_of, total, most, lean):
    weights = [(1 << 20) // math.isqrt(grade ** lean) + 1 for grade in range(2, number_of + 1)]
    rest, counts = total - most - (number_of - 1), [1] * (number_of - 1)
    while rest > 0:
        free = [i for i in range(number_of - 1) if counts[i] < most]
        pool, left = sum([weights[i] for i in free]), rest
        for i in free:
            more = min(most - counts[i], max(1, left * weights[i] // pool), rest)
            counts[i] = counts[i] + more
            rest = rest - more
    return np.array([most] + counts)


def uneven_parts(stream_key, count, total, most, skew):
    if count == 2:
        one = jax.random.randint(stream_key, (), max(1, total - most), min(most, total - 1) + 1)
        return jnp.stack([one, total - one])
    tallies = jnp.asarray(length_profile(count, total, most, skew), jnp.int32)
    couples = (count - 1) // 2
    giver, taker = tallies[1:1 + 2 * couples:2], tallies[2:2 + 2 * couples:2]
    margin = jnp.minimum(giver - 1, most - taker)
    shifted = jax.random.randint(jax.random.fold_in(stream_key, 1), (couples,), 0, 1 << 20) % (margin + 1)
    tallies = tallies.at[1:1 + 2 * couples:2].set(giver - shifted).at[2:2 + 2 * couples:2].set(taker + shifted)
    return tallies[jax.random.permutation(jax.random.fold_in(stream_key, 2), count)]


def deal_out(key, own, number, rows, count, top, reach, slope):
    sequence = jax.random.permutation(key, count)
    crowded, usual = portions_of(count, rows * top, reach, slope, True), portions_of(count, rows * top, reach, slope, False)
    places = jnp.arange(count)

    def named(sizes, turn):
        used = int((sizes > 0).sum())
        fixed = max(1, used // 4)
        moved = fixed + (places - fixed + turn * (used - fixed)) % max(1, count - fixed)
        return jnp.zeros((count,), jnp.int32).at[sequence[jnp.where(places < fixed, places, moved)]].set(jnp.asarray(sizes, jnp.int32))

    sizes = jnp.where(number % 4 == 0, named(crowded, number // 4), named(usual, number - number // 4 - 1))
    mixed = jax.random.permutation(jax.random.fold_in(own, 3), count)
    source_of, taker = mixed[0:count // 2 * 2:2], mixed[1:count // 2 * 2:2]
    room = jnp.minimum(sizes[source_of] - 1, reach - sizes[taker]) // 2
    room = jnp.where((source_of == sequence[0]) | (taker == sequence[0]) | (sizes[taker] == 0), 0, jnp.maximum(room, 0))
    moved = jax.random.randint(jax.random.fold_in(own, 4), (count // 2,), 0, 1 << 20) % (room + 1)
    sizes = sizes.at[source_of].add(-moved).at[taker].add(moved)
    items = jnp.searchsorted(jnp.cumsum(sizes), jnp.arange(rows * top), side="right").astype(jnp.int32)
    grid = items.reshape(top, rows).T
    grid = grid[jax.random.permutation(jax.random.fold_in(own, 1), rows)]
    turn = jax.random.randint(jax.random.fold_in(own, 2), (rows, 1), 0, top)
    return jnp.take_along_axis(grid, (jnp.arange(top)[None, :] + turn) % top, axis=1)


def portions_of(amount, total, bound, lean, full):
    loads = [(1 << 20) // math.isqrt(rank ** lean) + 1 for rank in range(1, amount + 1)]
    largest = bound if full else min(bound, max(-(-total // amount), total * loads[0] // sum(loads)))
    least = 1 if total - largest >= amount - 1 else 0
    counts, rest = [largest] + [least] * (amount - 1), total - largest - least * (amount - 1)
    while rest > 0:
        candidates = [i for i in range(1, amount) if counts[i] < largest] or [i for i in range(1, amount) if counts[i] < bound]
        pool, left = sum([loads[i] for i in candidates]), rest
        for i in candidates:
            extra = min(bound - counts[i], max(1, left * loads[i] // pool), rest)
            counts[i] = counts[i] + extra
            rest = rest - extra
    return np.array(counts)


def bell_draw(rng, shape, deviation, limit, cuts=(), kind=jnp.bfloat16):
    gain = steps_of(rng, shape, cuts, -0.22, 0.18) if cuts else 1.0
    array = jax.random.normal(rng, shape, jnp.float32) * deviation * gain
    return jnp.minimum(jnp.maximum(array, -limit), limit).astype(kind)


def setup_inputs(seed: int = 0) -> dict:
    arg_keys = jax.random.split(jax.random.key(seed), 12)
    queries = draw_queries(jax.random.fold_in(arg_keys[11], 71), 0)
    keys = draw_keys(jax.random.fold_in(arg_keys[11], 71), 0)
    values = bell_draw(arg_keys[2], (TOKEN_COUNT, KEY_HEADS * HEAD_WIDTH), 1.0, 6.0, ((0, 256),))
    lengths = jax.vmap(lambda own: uneven_parts(own, ROLLOUTS, REPLICA_TOKENS, CONTEXT_TOKENS, 2))(jax.random.split(arg_keys[3], N_DP)).reshape((N_DP, ROLLOUTS)).astype(jnp.int32)
    hidden = bell_draw(arg_keys[4], (TOKEN_COUNT, D), 1.0, 6.0, ((0, 256),))
    norm_gain = jnp.clip(1.0 + 0.18 * jax.random.normal(arg_keys[5], (D,), jnp.float32), 0.1, 1.9)
    routes_keys = jax.random.split(jax.random.fold_in(arg_keys[6], 1), TOKEN_COUNT // DEVICE_TOKENS)
    routes_turns = jax.random.permutation(jax.random.fold_in(arg_keys[6], 3), TOKEN_COUNT // DEVICE_TOKENS)
    routes = jax.vmap(lambda own, number: deal_out(jax.random.fold_in(arg_keys[6], 2), own, number, DEVICE_TOKENS, EXPERTS, TOPK, CAP, 2))(routes_keys, routes_turns).reshape((TOKEN_COUNT, TOPK))
    gates = jnp.clip(jnp.exp(math.log(1.0) - 1.609438 * jax.random.uniform(arg_keys[7], (TOKEN_COUNT, TOPK), jnp.float32) ** steps_of(arg_keys[7], (TOKEN_COUNT, TOPK), ((0, 256),), -0.2, 0.2)), 0.2, 1.0)
    w_gate = bell_draw(arg_keys[8], (EXPERTS, D, FF), D ** -0.5, 0.09375, ((0, 16), (2, 16)))
    w_up = bell_draw(arg_keys[9], (EXPERTS, D, FF), D ** -0.5, 0.09375, ((0, 16), (2, 16)))
    w_down = bell_draw(arg_keys[10], (EXPERTS, D, FF), FF ** -0.5, 0.21875, ((0, 16), (2, 16)))
    return dict(queries=queries, keys=keys, values=values, lengths=lengths, hidden=hidden, norm_gain=norm_gain, routes=routes, gates=gates, w_gate=w_gate, w_up=w_up, w_down=w_down)


def rollout_of(positions, bounds):
    return lax.optimization_barrier(jnp.sum((positions[:, None] >= bounds[None, :]).astype(jnp.int32), axis=1))

def reference(queries, keys, values, lengths, hidden, norm_gain, routes, gates, w_gate, w_up, w_down):
    head_grouping = QUERY_HEADS // KEY_HEADS
    scaling = 1.0 / math.sqrt(HEAD_WIDTH)
    contexts = []
    for rollout_set in range(N_DP):
        leading_row = rollout_set * REPLICA_TOKENS
        query_heads = queries[leading_row:leading_row + REPLICA_TOKENS].reshape(REPLICA_TOKENS, KEY_HEADS, head_grouping, HEAD_WIDTH)
        stacked_rows = jnp.stack((keys[leading_row:leading_row + REPLICA_TOKENS], values[leading_row:leading_row + REPLICA_TOKENS]))
        stacked_rows = jnp.concatenate((jnp.zeros((2, CONTEXT_TOKENS, KEY_HEADS * HEAD_WIDTH), stacked_rows.dtype), stacked_rows), axis=1)
        bounds = jnp.cumsum(lengths[rollout_set])

        def one_block(block_index, query_heads=query_heads, stacked_rows=stacked_rows, bounds=bounds):
            offset = block_index * DEVICE_TOKENS
            query_block = lax.dynamic_slice_in_dim(query_heads, offset, DEVICE_TOKENS, 0).astype(jnp.float32)
            current_key_block = lax.dynamic_slice_in_dim(stacked_rows, offset, CONTEXT_TOKENS + DEVICE_TOKENS, 1)
            query_pos = offset + jnp.arange(DEVICE_TOKENS, dtype=jnp.int32)
            key_pos = offset - CONTEXT_TOKENS + jnp.arange(CONTEXT_TOKENS + DEVICE_TOKENS, dtype=jnp.int32)
            visible = (key_pos[None, :] <= query_pos[:, None]) & (key_pos[None, :] >= 0)
            visible = visible & (rollout_of(key_pos, bounds)[None, :] == rollout_of(query_pos, bounds)[:, None])
            key_head_rows = current_key_block[0].reshape(CONTEXT_TOKENS + DEVICE_TOKENS, KEY_HEADS, HEAD_WIDTH).astype(jnp.float32)
            value_head_rows = current_key_block[1].reshape(CONTEXT_TOKENS + DEVICE_TOKENS, KEY_HEADS, HEAD_WIDTH).astype(jnp.float32)
            scores = jnp.einsum('tkgd,skd->tkgs', query_block, key_head_rows) * scaling
            wide_mask = visible[:, None, None, :]
            scores = jnp.where(wide_mask, scores, -1e+30)
            row_max = lax.optimization_barrier(jnp.max(scores, axis=-1, keepdims=True))
            probs = jnp.where(wide_mask, jnp.exp(scores - row_max), 0.0)
            row_total = lax.optimization_barrier(jnp.sum(probs, axis=-1))
            rounded = lax.optimization_barrier(probs.astype(jnp.bfloat16)).astype(jnp.float32)
            summed = jnp.einsum('tkgs,skd->tkgd', rounded, value_head_rows)
            return (summed / row_total[..., None]).reshape(DEVICE_TOKENS, QUERY_HEADS * HEAD_WIDTH).astype(jnp.bfloat16)
        blocks = lax.map(one_block, jnp.arange(REPLICA_TOKENS // DEVICE_TOKENS, dtype=jnp.int32))
        contexts.append(blocks.reshape(REPLICA_TOKENS, QUERY_HEADS * HEAD_WIDTH))
    context = jnp.concatenate(contexts, axis=0)
    hidden_f = hidden.astype(jnp.float32)
    normed = (hidden_f * lax.rsqrt(lax.optimization_barrier(jnp.mean(hidden_f * hidden_f, axis=-1, keepdims=True)) + 1e-06) * norm_gain.astype(jnp.float32)).astype(jnp.bfloat16)
    padded_rows = jnp.concatenate((normed, jnp.zeros((1, D), jnp.bfloat16)))
    flat_routes = routes.reshape(-1)
    flat_gates = gates.reshape(-1).astype(jnp.float32)
    owner_tokens = jnp.arange(TOKEN_COUNT * TOPK, dtype=jnp.int32) // TOPK
    capacity = N_DP * N_CTX * N_EXP * CAP

    def one_expert(running, expert_id):
        route_hit = flat_routes == expert_id
        route_rank = jnp.cumsum(route_hit.astype(jnp.int32)) - 1
        slot_target = jnp.where(route_hit, route_rank, capacity).astype(jnp.int32)
        members = jnp.full((capacity,), TOKEN_COUNT, jnp.int32).at[slot_target].set(owner_tokens, mode='drop')
        slot_gates = jnp.zeros((capacity,), jnp.float32).at[slot_target].set(flat_gates, mode='drop')
        expert_rows = padded_rows[members]
        gate_mat = lax.dynamic_index_in_dim(w_gate, expert_id, 0, keepdims=False)
        up_mat = lax.dynamic_index_in_dim(w_up, expert_id, 0, keepdims=False)
        down_mat = lax.dynamic_index_in_dim(w_down, expert_id, 0, keepdims=False)
        gate_part = jnp.dot(expert_rows, gate_mat, preferred_element_type=jnp.float32)
        up_part = jnp.dot(expert_rows, up_mat, preferred_element_type=jnp.float32)
        active = (jax.nn.silu(gate_part) * up_part).astype(jnp.bfloat16)
        result = lax.dot_general(active, down_mat, (((1,), (1,)), ((), ())), preferred_element_type=jnp.float32).astype(jnp.bfloat16)
        running = running.at[members].add(slot_gates[:, None] * result.astype(jnp.float32), mode='drop')
        return (running, None)
    mixture, _ = lax.scan(one_expert, jnp.zeros((TOKEN_COUNT, D), jnp.float32), jnp.arange(EXPERTS, dtype=jnp.int32))
    return (context, mixture.astype(jnp.bfloat16))
```

```python
import functools
import math

import jax
import jax.numpy as jnp
from jax import lax
from jax.experimental import pallas as pl
from jax.experimental.pallas import tpu as pltpu
from jax.sharding import PartitionSpec as P

MESH = pl.DeviceIdType.MESH
HEAD_WIDTH = 128
QUERY_HEADS = 32
KEY_HEADS = 2
SIDE = 4
DEPTH = 8
QUARTERS = 4
CAP = 24


def place():
    dp, ctx, ex = lax.axis_index("dp"), lax.axis_index("ctx"), lax.axis_index("exp")
    return (ctx % 2) * 2 + dp, ctx // 2, ex // 2, ex % 2


def device_at(x, y, ex):
    return (x % 2, y * 2 + x // 2, ex)


def slot_hits(routes):
    experts, tokens = 16, routes.shape[1]
    ids = lax.broadcasted_iota(jnp.int32, (experts, tokens), 0)
    hits = ((ids == routes[0:1, :]) | (ids == routes[1:2, :])).astype(jnp.float32)
    earlier = (
        lax.broadcasted_iota(jnp.int32, (tokens, tokens), 0)
        < lax.broadcasted_iota(jnp.int32, (tokens, tokens), 1)
    ).astype(jnp.bfloat16)
    ranks = jnp.dot(hits.astype(jnp.bfloat16), earlier, preferred_element_type=jnp.float32)
    ranks = jnp.where(hits > 0, ranks, -1.0).astype(jnp.int32)
    wanted = lax.broadcasted_iota(jnp.int32, (experts, CAP, tokens), 1)
    return (ranks[:, None, :] == wanted).astype(jnp.float32)


def exchange_kernel(
    w_gate, w_up, w_down, keys, values, hidden, gain, routes,
    wall, arrived, window,
    hidden_rows, packed,
    local_sem, out_sem, in_sem, route_out, route_in, kv_out, kv_in,
):
    x, y, z, core = place()
    dp, ctx, ex = lax.axis_index("dp"), lax.axis_index("ctx"), lax.axis_index("exp")
    right, left = lax.rem(x + 1, SIDE), lax.rem(x + SIDE - 1, SIDE)
    above, below = lax.rem(y + 1, SIDE), lax.rem(y + SIDE - 1, SIDE)
    across, over = lax.rem(x + 2, SIDE), lax.rem(y + 2, SIDE)
    to_right, to_left = device_at(right, y, ex), device_at(left, y, ex)
    to_above, to_below = device_at(x, above, ex), device_at(x, below, ex)
    next_ctx, prior_ctx = lax.rem(ctx + 1, 8), lax.rem(ctx + 7, 8)
    sibling = z * 2 + 1 - core

    hidden_copy = pltpu.make_async_copy(hidden, hidden_rows, local_sem.at[14])
    hidden_copy.start()
    quarter = wall.shape[-1]
    mine = y * SIDE + x
    local = []
    for m, source in enumerate((w_gate, w_up, w_down)):
        for q in range(QUARTERS):
            copy = pltpu.make_async_copy(
                source.at[:, pl.ds(q * quarter, quarter)], wall.at[m, q, mine], local_sem.at[m * QUARTERS + q]
            )
            copy.start()
            local.append(copy)
    width = keys.shape[1]
    key_copy = pltpu.make_async_copy(keys, window.at[DEPTH, core, :, pl.ds(0, width)], local_sem.at[12])
    value_copy = pltpu.make_async_copy(values, window.at[DEPTH, core, :, pl.ds(width, width)], local_sem.at[13])
    key_copy.start()
    value_copy.start()

    barrier = pltpu.get_barrier_semaphore()
    for neighbour in (to_right, to_left, to_above, to_below):
        pl.semaphore_signal(barrier, inc=1, device_id=neighbour, device_id_type=MESH)
    for step in range(1, 16):
        pl.semaphore_signal(barrier, inc=1, device_id=(dp, ctx, lax.rem(ex + step, 16)), device_id_type=MESH)
    for plane in range(DEPTH):
        pl.semaphore_signal(barrier, inc=1, device_id=(dp, prior_ctx, plane * 2 + core), device_id_type=MESH)
    pl.semaphore_wait(barrier, 4 + 15 + DEPTH)

    sent = []
    counts = [0, 0, 0]

    def send(m, first, count, shard, target):
        part = wall.at[m, pl.ds(first, count), shard]
        copy = pltpu.make_async_remote_copy(
            src_ref=part, dst_ref=part,
            send_sem=out_sem.at[m, counts[m]], recv_sem=in_sem.at[m, shard, first],
            device_id=target, device_id_type=MESH,
        )
        counts[m] += 1
        copy.start()
        sent.append(copy)

    def landed(m, first, count, shard):
        part = wall.at[m, pl.ds(first, count), shard]
        pltpu.make_async_copy(part, part, in_sem.at[m, shard, first]).wait()

    def at(shard_x, shard_y):
        return shard_y * SIDE + shard_x

    for m in range(3):
        for copy in local[m * QUARTERS:(m + 1) * QUARTERS]:
            copy.wait()
        for target in (to_right, to_left, to_above, to_below):
            send(m, 0, 4, mine, target)

    key_copy.wait()
    value_copy.wait()
    kv_copies = []
    for step in range(DEPTH):
        plane = lax.rem(z + step, DEPTH)
        if step == 0:
            target_ctx = next_ctx
        else:
            target_ctx = lax.rem(ctx + (z + step) // DEPTH, 8)
        copy = pltpu.make_async_remote_copy(
            src_ref=window.at[DEPTH, core], dst_ref=window.at[(DEPTH - step) % DEPTH, core],
            send_sem=kv_out.at[step], recv_sem=kv_in.at[(DEPTH - step) % DEPTH],
            device_id=(dp, target_ctx, plane * 2 + core), device_id_type=MESH,
        )
        copy.start()
        kv_copies.append(copy)

    hidden_copy.wait()
    picks = slot_hits(routes[...]).reshape(16 * CAP, -1).astype(jnp.bfloat16)
    rows = hidden_rows[...].astype(jnp.float32)
    scale = lax.rsqrt(jnp.mean(rows * rows, axis=-1, keepdims=True) + 1e-06)
    for q in range(QUARTERS):
        cols = pl.ds(q * quarter, quarter)
        normed = (hidden_rows[:, cols].astype(jnp.float32) * scale * gain[:, cols]).astype(jnp.bfloat16)
        block = jnp.dot(picks, normed, preferred_element_type=jnp.float32).astype(jnp.bfloat16)
        packed[:, :, cols] = block.reshape(16, CAP, quarter)
    own_rows = pltpu.make_async_copy(packed.at[ex], arrived.at[ex], local_sem.at[15])
    own_rows.start()
    route_copies = []
    for step in (8, 7, 9, 6, 10, 5, 11, 4, 12, 3, 13, 2, 14, 1, 15):
        peer = lax.rem(ex + step, 16)
        copy = pltpu.make_async_remote_copy(
            src_ref=packed.at[peer], dst_ref=arrived.at[ex],
            send_sem=route_out.at[step - 1], recv_sem=route_in.at[ex],
            device_id=(dp, ctx, peer), device_id_type=MESH,
        )
        copy.start()
        route_copies.append(copy)

    for m in range(3):
        landed(m, 0, 4, at(left, y))
        send(m, 0, 2, at(left, y), to_right)
        send(m, 1, 2, at(left, y), to_above)
        send(m, 1, 2, at(left, y), to_below)
        landed(m, 0, 4, at(right, y))
        send(m, 2, 2, at(right, y), to_left)
        send(m, 1, 2, at(right, y), to_above)
        send(m, 1, 2, at(right, y), to_below)
        landed(m, 0, 4, at(x, below))
        send(m, 0, 2, at(x, below), to_above)
        for q in (0, 3):
            send(m, q, 1, at(x, below), to_right)
            send(m, q, 1, at(x, below), to_left)
        landed(m, 0, 4, at(x, above))
        send(m, 2, 2, at(x, above), to_below)
        for q in (0, 3):
            send(m, q, 1, at(x, above), to_right)
            send(m, q, 1, at(x, above), to_left)

    for m in range(3):
        landed(m, 0, 2, at(across, y))
        send(m, 1, 1, at(across, y), to_above)
        send(m, 1, 1, at(across, y), to_below)
        landed(m, 2, 2, at(across, y))
        send(m, 2, 1, at(across, y), to_above)
        send(m, 2, 1, at(across, y), to_below)
        landed(m, 0, 2, at(x, over))
        send(m, 0, 1, at(x, over), to_right)
        send(m, 0, 1, at(x, over), to_left)
        landed(m, 2, 2, at(x, over))
        send(m, 3, 1, at(x, over), to_right)
        send(m, 3, 1, at(x, over), to_left)
        for side in (left, right):
            landed(m, 1, 2, at(side, below))
            send(m, 1, 1, at(side, below), to_above)
            landed(m, 1, 2, at(side, above))
            send(m, 2, 1, at(side, above), to_below)
        for side in (below, above):
            landed(m, 0, 1, at(left, side))
            landed(m, 3, 1, at(left, side))
            send(m, 0, 1, at(left, side), to_right)
            landed(m, 0, 1, at(right, side))
            landed(m, 3, 1, at(right, side))
            send(m, 3, 1, at(right, side), to_left)

    for slot in range(DEPTH):
        pltpu.make_async_copy(window.at[slot, core], window.at[slot, core], kv_in.at[slot]).wait()
    share = pltpu.make_async_remote_copy(
        src_ref=window.at[:, core], dst_ref=window.at[:, core],
        send_sem=kv_out.at[DEPTH], recv_sem=kv_in.at[DEPTH],
        device_id=(dp, ctx, sibling), device_id_type=MESH,
    )
    share.start()

    for m in range(3):
        landed(m, 1, 1, at(across, below))
        landed(m, 2, 1, at(across, below))
        send(m, 1, 1, at(across, below), to_above)
        landed(m, 1, 1, at(across, above))
        landed(m, 2, 1, at(across, above))
        send(m, 2, 1, at(across, above), to_below)
        landed(m, 0, 1, at(left, over))
        landed(m, 3, 1, at(left, over))
        send(m, 0, 1, at(left, over), to_right)
        landed(m, 0, 1, at(right, over))
        landed(m, 3, 1, at(right, over))
        send(m, 3, 1, at(right, over), to_left)

    own_rows.wait()
    for step in range(1, 16):
        peer = lax.rem(ex + step, 16)
        pltpu.make_async_copy(arrived.at[peer], arrived.at[peer], route_in.at[peer]).wait()
    for m in range(3):
        for side in (left, right):
            landed(m, 1, 1, at(side, over))
            landed(m, 2, 1, at(side, over))
        for side in (below, above):
            landed(m, 0, 1, at(across, side))
            landed(m, 3, 1, at(across, side))
        for q in range(QUARTERS):
            landed(m, q, 1, at(across, over))
    pltpu.make_async_copy(window.at[:, 1 - core], window.at[:, 1 - core], kv_in.at[DEPTH]).wait()
    share.wait_send()
    for copy in kv_copies + route_copies + sent:
        copy.wait_send()


def exchange(w_gate, w_up, w_down, keys, values, hidden, gain, routes):
    tokens, width = hidden.shape
    piece = w_gate.shape[0]
    anywhere, vmem = pl.BlockSpec(memory_space=pl.ANY), pl.BlockSpec(memory_space=pltpu.VMEM)
    bf16, dma = jnp.bfloat16, pltpu.SemaphoreType.DMA
    return pl.pallas_call(
        exchange_kernel,
        out_shape=(
            jax.ShapeDtypeStruct((3, QUARTERS, SIDE * SIDE, piece, width // QUARTERS), bf16),
            jax.ShapeDtypeStruct((16, CAP, width), bf16),
            jax.ShapeDtypeStruct((DEPTH + 1, 2, tokens, 2 * keys.shape[1]), bf16),
        ),
        in_specs=[anywhere] * 6 + [vmem] * 2,
        out_specs=[anywhere] * 3,
        scratch_shapes=[
            pltpu.VMEM((tokens, width), bf16),
            pltpu.VMEM((16, CAP, width), bf16),
            dma((16,)), dma((3, 40)), dma((3, 16, 4)), dma((15,)), dma((16,)), dma((9,)), dma((9,)),
        ],
        compiler_params=pltpu.CompilerParams(
            collective_id=0, has_side_effects=True, vmem_limit_bytes=40 * 1024 * 1024
        ),
        cost_estimate=pl.CostEstimate(flops=10**9, bytes_accessed=40 * 10**6, transcendentals=0),
        name="exchange",
    )(w_gate, w_up, w_down, keys, values, hidden, gain, routes)


def expert_kernel(rows, gate, up, down, out, gate_sum, up_sum, active):
    i = pl.program_id(0)
    turned = (((1,), (1,)), ((), ()))

    @pl.when(i == 0)
    def _():
        gate_sum[...] = jnp.zeros_like(gate_sum)
        up_sum[...] = jnp.zeros_like(up_sum)

    @pl.when(i < QUARTERS)
    def _():
        gate_sum[...] += lax.dot_general(rows[...], gate[0, 0], turned, preferred_element_type=jnp.float32)
        up_sum[...] += lax.dot_general(rows[...], up[0, 0], turned, preferred_element_type=jnp.float32)

    @pl.when(i == QUARTERS - 1)
    def _():
        g = gate_sum[...]
        active[...] = (g / (1.0 + jnp.exp(-g)) * up_sum[...]).astype(jnp.bfloat16)

    @pl.when(i >= QUARTERS)
    def _():
        out[...] = jnp.dot(active[...], down[0, 0], preferred_element_type=jnp.float32).astype(out.dtype)


def expert_block(rows, wall):
    count, width = rows.shape
    units, quarter = wall.shape[2], wall.shape[3]
    early = lambda i: jnp.minimum(i, QUARTERS - 1)
    late = lambda i: jnp.maximum(i - QUARTERS, 0)
    block = (1, 1, units, quarter)
    return pl.pallas_call(
        expert_kernel,
        grid=(2 * QUARTERS,),
        out_shape=jax.ShapeDtypeStruct((count, width), jnp.bfloat16),
        in_specs=[
            pl.BlockSpec((count, quarter), lambda i: (0, early(i))),
            pl.BlockSpec(block, lambda i: (0, early(i), 0, 0)),
            pl.BlockSpec(block, lambda i: (1, early(i), 0, 0)),
            pl.BlockSpec(block, lambda i: (2, late(i), 0, 0)),
        ],
        out_specs=pl.BlockSpec((count, quarter), lambda i: (0, late(i))),
        scratch_shapes=[
            pltpu.VMEM((count, units), jnp.float32),
            pltpu.VMEM((count, units), jnp.float32),
            pltpu.VMEM((count, units), jnp.bfloat16),
        ],
        compiler_params=pltpu.CompilerParams(vmem_limit_bytes=40 * 1024 * 1024),
        cost_estimate=pl.CostEstimate(flops=7 * 10**9, bytes_accessed=25 * 10**6, transcendentals=0),
        name="experts",
    )(rows, wall, wall, wall)


HEADS_AT_ONCE = 4


def attention_kernel(lengths, queries, window, out, bias):
    i = pl.program_id(0)
    tokens, keys = queries.shape[0], window.shape[0]
    ctx, ex = lax.axis_index("ctx"), lax.axis_index("exp")

    @pl.when(i == 0)
    def _():
        query_pos = (ctx * 16 + ex) * tokens + lax.broadcasted_iota(jnp.int32, (tokens, 1), 0)
        begin = jnp.zeros_like(query_pos)
        bound = jnp.int32(0)
        for r in range(lengths.shape[1]):
            bound = bound + lengths[0, r]
            begin = jnp.where(query_pos >= bound, bound, begin)
        step = 256
        for c in range(keys // step):
            key_pos = (
                ctx * 16 + (ex // 2) * 2 - 16
            ) * tokens + c * step + lax.broadcasted_iota(jnp.int32, (tokens, step), 1)
            seen = (key_pos <= query_pos) & (key_pos >= begin)
            bias[:, c * step:(c + 1) * step] = jnp.where(seen, 0.0, -1e30)

    group = i // (QUERY_HEADS // KEY_HEADS // HEADS_AT_ONCE)
    key_col = pl.multiple_of(group * HEAD_WIDTH, HEAD_WIDTH)
    value_col = pl.multiple_of((KEY_HEADS + group) * HEAD_WIDTH, HEAD_WIDTH)
    key_rows = window[:, pl.ds(key_col, HEAD_WIDTH)]
    value_rows = window[:, pl.ds(value_col, HEAD_WIDTH)]
    stacked = jnp.concatenate(
        [queries[:, h * HEAD_WIDTH:(h + 1) * HEAD_WIDTH] for h in range(HEADS_AT_ONCE)], axis=0
    )
    scores = lax.dot_general(stacked, key_rows, (((1,), (1,)), ((), ())), preferred_element_type=jnp.float32)
    scores = scores.reshape(HEADS_AT_ONCE, tokens, keys) + bias[...][None]
    top = jnp.max(scores, axis=-1, keepdims=True)
    probs = jnp.exp2((scores - top) * (math.log2(math.e) / math.sqrt(HEAD_WIDTH)))
    total = jnp.sum(probs, axis=-1, keepdims=True)
    summed = jnp.dot(
        probs.reshape(HEADS_AT_ONCE * tokens, keys).astype(jnp.bfloat16), value_rows,
        preferred_element_type=jnp.float32,
    ).reshape(HEADS_AT_ONCE, tokens, HEAD_WIDTH)
    result = (summed / total).astype(out.dtype)
    for h in range(HEADS_AT_ONCE):
        out[:, h * HEAD_WIDTH:(h + 1) * HEAD_WIDTH] = result[h]


def attend(lengths, queries, window):
    tokens, width = queries.shape
    columns = HEADS_AT_ONCE * HEAD_WIDTH
    return pl.pallas_call(
        attention_kernel,
        grid=(width // columns,),
        out_shape=jax.ShapeDtypeStruct((tokens, width), jnp.bfloat16),
        in_specs=[
            pl.BlockSpec(memory_space=pltpu.SMEM),
            pl.BlockSpec((tokens, columns), lambda i: (0, i)),
            pl.BlockSpec(window.shape, lambda i: (0, 0)),
        ],
        out_specs=pl.BlockSpec((tokens, columns), lambda i: (0, i)),
        scratch_shapes=[pltpu.VMEM((tokens, window.shape[0]), jnp.float32)],
        compiler_params=pltpu.CompilerParams(vmem_limit_bytes=40 * 1024 * 1024),
        cost_estimate=pl.CostEstimate(
            flops=20 * 10**9, bytes_accessed=10 * 10**6, transcendentals=10**7
        ),
        name="attention",
    )(lengths, queries, window)


def mix_kernel(routes, gates, returned, out):
    experts, tokens = 16, routes.shape[1]
    ids = lax.broadcasted_iota(jnp.int32, (experts, tokens), 0)
    weight = jnp.where(ids == routes[0:1, :], gates[0:1, :], 0.0)
    weight = weight + jnp.where(ids == routes[1:2, :], gates[1:2, :], 0.0)
    spread = (slot_hits(routes[...]) * weight[:, None, :]).reshape(experts * CAP, tokens)
    high = spread.astype(jnp.bfloat16)
    low = (spread - high.astype(jnp.float32)).astype(jnp.bfloat16)
    across = (((0,), (0,)), ((), ()))
    rows = returned[...]
    total = lax.dot_general(high, rows, across, preferred_element_type=jnp.float32)
    total = total + lax.dot_general(low, rows, across, preferred_element_type=jnp.float32)
    out[...] = total.astype(out.dtype)


def mix(routes, gates, returned):
    count, width = returned.shape
    tokens, quarter = routes.shape[1], width // QUARTERS
    return pl.pallas_call(
        mix_kernel,
        grid=(QUARTERS,),
        out_shape=jax.ShapeDtypeStruct((tokens, width), jnp.bfloat16),
        in_specs=[
            pl.BlockSpec((2, tokens), lambda i: (0, 0)),
            pl.BlockSpec((2, tokens), lambda i: (0, 0)),
            pl.BlockSpec((count, quarter), lambda i: (0, i)),
        ],
        out_specs=pl.BlockSpec((tokens, quarter), lambda i: (0, i)),
        compiler_params=pltpu.CompilerParams(vmem_limit_bytes=32 * 1024 * 1024),
        cost_estimate=pl.CostEstimate(flops=10**9, bytes_accessed=4 * 10**6, transcendentals=0),
        name="mix",
    )(routes, gates, returned)


def shards(queries, keys, values, lengths, hidden, norm_gain, routes, gates, w_gate, w_up, w_down):
    width = hidden.shape[1]
    turned = [jnp.swapaxes(w[0], 0, 1) for w in (w_gate, w_up, w_down)]
    wall, arrived, window = exchange(*turned, keys, values, hidden, norm_gain[None, :], routes.T)
    units = SIDE * SIDE * turned[0].shape[0]
    results = expert_block(arrived.reshape(16 * CAP, width), wall.reshape(3, QUARTERS, units, width // QUARTERS))
    returned = lax.all_to_all(results.reshape(16, CAP, width), "exp", split_axis=0, concat_axis=0, tiled=True)
    context = attend(lengths, queries, window.reshape(-1, window.shape[-1]))
    expert_mix = mix(routes.T, gates.T, returned.reshape(16 * CAP, width))
    return context, expert_mix


def solution(mesh):
    whole = P(("dp", "ctx", "exp"), None)
    weights = P("exp", None, ("dp", "ctx"))
    return jax.shard_map(
        shards,
        mesh=mesh,
        in_specs=(whole, whole, whole, P("dp", None), whole, P(), whole, whole, weights, weights, weights),
        out_specs=(whole, whole),
        check_vma=False,
    )
```

```python
import math

import jax
import jax.numpy as jnp
from jax import lax
from jax.experimental import pallas as pl
from jax.experimental.pallas import tpu as pltpu
from jax.sharding import PartitionSpec as P

MESH = pl.DeviceIdType.MESH
HEAD_WIDTH = 128
QUERY_HEADS = 32
KEY_HEADS = 2
SIDE = 4
DEPTH = 8
QUARTERS = 4
CAP = 24
HEADS_AT_ONCE = 4
TURNED = (((1,), (1,)), ((), ()))


def place():
    dp, ctx, ex = lax.axis_index("dp"), lax.axis_index("ctx"), lax.axis_index("exp")
    return (ctx % 2) * 2 + dp, ctx // 2, ex // 2, ex % 2


def device_at(x, y, ex):
    return (x % 2, y * 2 + x // 2, ex)


def slot_hits(routes):
    experts, tokens = 16, routes.shape[1]
    ids = lax.broadcasted_iota(jnp.int32, (experts, tokens), 0)
    hits = ((ids == routes[0:1, :]) | (ids == routes[1:2, :])).astype(jnp.float32)
    earlier = (
        lax.broadcasted_iota(jnp.int32, (tokens, tokens), 0)
        < lax.broadcasted_iota(jnp.int32, (tokens, tokens), 1)
    ).astype(jnp.bfloat16)
    ranks = jnp.dot(hits.astype(jnp.bfloat16), earlier, preferred_element_type=jnp.float32)
    ranks = jnp.where(hits > 0, ranks, -1.0).astype(jnp.int32)
    wanted = lax.broadcasted_iota(jnp.int32, (experts, CAP, tokens), 1)
    return (ranks[:, None, :] == wanted).astype(jnp.float32)


def attention_bias(lengths, tokens, bias):
    ctx, ex = lax.axis_index("ctx"), lax.axis_index("exp")
    query_pos = (ctx * 16 + ex) * tokens + lax.broadcasted_iota(jnp.int32, (tokens, 1), 0)
    begin = jnp.zeros_like(query_pos)
    bound = jnp.int32(0)
    for r in range(lengths.shape[1]):
        bound = bound + lengths[0, r]
        begin = jnp.where(query_pos >= bound, bound, begin)
    first = (ctx * 16 + (ex // 2) * 2 - 16) * tokens
    step = 256
    for c in range(bias.shape[1] // step):
        key_pos = first + c * step + lax.broadcasted_iota(jnp.int32, (tokens, step), 1)
        seen = (key_pos <= query_pos) & (key_pos >= begin)
        bias[:, c * step:(c + 1) * step] = jnp.where(seen, 0.0, -1e30)


def attend(i, queries, window, bias, out):
    tokens, keys = bias.shape
    columns = HEADS_AT_ONCE * HEAD_WIDTH
    place_of = pl.multiple_of(i * columns, columns)
    group = i // (QUERY_HEADS // KEY_HEADS // HEADS_AT_ONCE)
    key_col = pl.multiple_of(group * HEAD_WIDTH, HEAD_WIDTH)
    value_col = pl.multiple_of((KEY_HEADS + group) * HEAD_WIDTH, HEAD_WIDTH)
    key_rows = window[:, :, :, pl.ds(key_col, HEAD_WIDTH)].reshape(keys, HEAD_WIDTH)
    value_rows = window[:, :, :, pl.ds(value_col, HEAD_WIDTH)].reshape(keys, HEAD_WIDTH)
    block = queries[:, pl.ds(place_of, columns)]
    stacked = jnp.concatenate(
        [block[:, h * HEAD_WIDTH:(h + 1) * HEAD_WIDTH] for h in range(HEADS_AT_ONCE)], axis=0
    )
    scores = lax.dot_general(stacked, key_rows, TURNED, preferred_element_type=jnp.float32)
    scores = scores.reshape(HEADS_AT_ONCE, tokens, keys) + bias[...][None]
    top = jnp.max(scores, axis=-1, keepdims=True)
    probs = jnp.exp2((scores - top) * (math.log2(math.e) / math.sqrt(HEAD_WIDTH)))
    total = jnp.sum(probs, axis=-1, keepdims=True)
    summed = jnp.dot(
        probs.reshape(HEADS_AT_ONCE * tokens, keys).astype(jnp.bfloat16), value_rows,
        preferred_element_type=jnp.float32,
    ).reshape(HEADS_AT_ONCE, tokens, HEAD_WIDTH)
    result = (summed / total).astype(out.dtype)
    out[:, pl.ds(place_of, columns)] = jnp.concatenate([result[h] for h in range(HEADS_AT_ONCE)], axis=1)


def kernel(
    w_gate, w_up, w_down, queries, keys, values, hidden, gain, routes, gates, lengths,
    context, mixture,
    wall, window, hidden_rows, query_rows, packed, arrived, results, returned, sums, active, bias,
    local_sem, out_sem, in_sem, route_out, route_in, kv_out, kv_in, back_out, back_in, back_own,
):
    x, y, z, core = place()
    dp, ctx, ex = lax.axis_index("dp"), lax.axis_index("ctx"), lax.axis_index("exp")
    right, left = lax.rem(x + 1, SIDE), lax.rem(x + SIDE - 1, SIDE)
    above, below = lax.rem(y + 1, SIDE), lax.rem(y + SIDE - 1, SIDE)
    across, over = lax.rem(x + 2, SIDE), lax.rem(y + 2, SIDE)
    to_right, to_left = device_at(right, y, ex), device_at(left, y, ex)
    to_above, to_below = device_at(x, above, ex), device_at(x, below, ex)
    next_ctx, prior_ctx = lax.rem(ctx + 1, 8), lax.rem(ctx + 7, 8)
    sibling = z * 2 + 1 - core
    quarter = wall.shape[-1]
    count = arrived.shape[0] * arrived.shape[1]
    mine = y * SIDE + x

    local = []
    for m, source in enumerate((w_gate, w_up, w_down)):
        for q in range(QUARTERS):
            copy = pltpu.make_async_copy(
                source.at[:, pl.ds(q * quarter, quarter)], wall.at[m, q, mine], local_sem.at[m * QUARTERS + q]
            )
            copy.start()
            local.append(copy)
    width = keys.shape[1]
    key_copy = pltpu.make_async_copy(keys, window.at[DEPTH, core, :, pl.ds(0, width)], local_sem.at[12])
    value_copy = pltpu.make_async_copy(values, window.at[DEPTH, core, :, pl.ds(width, width)], local_sem.at[13])
    hidden_copy = pltpu.make_async_copy(hidden, hidden_rows, local_sem.at[14])
    query_copy = pltpu.make_async_copy(queries, query_rows, local_sem.at[15])
    for copy in (key_copy, value_copy, hidden_copy, query_copy):
        copy.start()

    barrier = pltpu.get_barrier_semaphore()
    for neighbour in (to_right, to_left, to_above, to_below):
        pl.semaphore_signal(barrier, inc=1, device_id=neighbour, device_id_type=MESH)
    for step in range(1, 16):
        pl.semaphore_signal(barrier, inc=1, device_id=(dp, ctx, lax.rem(ex + step, 16)), device_id_type=MESH)
    pl.semaphore_signal(barrier, inc=1, device_id=(dp, prior_ctx, ex), device_id_type=MESH)
    pl.semaphore_wait(barrier, 4 + 15 + 1)

    sent = []
    counts = [0, 0, 0]

    def send(m, first, number, shard, target):
        part = wall.at[m, pl.ds(first, number), shard]
        copy = pltpu.make_async_remote_copy(
            src_ref=part, dst_ref=part,
            send_sem=out_sem.at[m, counts[m]], recv_sem=in_sem.at[m, shard, first],
            device_id=target, device_id_type=MESH,
        )
        counts[m] += 1
        copy.start()
        sent.append(copy)

    def landed(m, first, number, shard):
        part = wall.at[m, pl.ds(first, number), shard]
        pltpu.make_async_copy(part, part, in_sem.at[m, shard, first]).wait()

    def at(shard_x, shard_y):
        return shard_y * SIDE + shard_x

    def first_round(m):
        for copy in local[m * QUARTERS:(m + 1) * QUARTERS]:
            copy.wait()
        for target in (to_right, to_left, to_above, to_below):
            send(m, 0, 4, mine, target)

    def second_round(m):
        landed(m, 0, 4, at(left, y))
        send(m, 0, 2, at(left, y), to_right)
        send(m, 1, 2, at(left, y), to_above)
        send(m, 1, 2, at(left, y), to_below)
        landed(m, 0, 4, at(right, y))
        send(m, 2, 2, at(right, y), to_left)
        send(m, 1, 2, at(right, y), to_above)
        send(m, 1, 2, at(right, y), to_below)
        landed(m, 0, 4, at(x, below))
        send(m, 0, 2, at(x, below), to_above)
        for q in (0, 3):
            send(m, q, 1, at(x, below), to_right)
            send(m, q, 1, at(x, below), to_left)
        landed(m, 0, 4, at(x, above))
        send(m, 2, 2, at(x, above), to_below)
        for q in (0, 3):
            send(m, q, 1, at(x, above), to_right)
            send(m, q, 1, at(x, above), to_left)

    def third_round(m):
        landed(m, 0, 2, at(across, y))
        send(m, 1, 1, at(across, y), to_above)
        send(m, 1, 1, at(across, y), to_below)
        landed(m, 2, 2, at(across, y))
        send(m, 2, 1, at(across, y), to_above)
        send(m, 2, 1, at(across, y), to_below)
        landed(m, 0, 2, at(x, over))
        send(m, 0, 1, at(x, over), to_right)
        send(m, 0, 1, at(x, over), to_left)
        landed(m, 2, 2, at(x, over))
        send(m, 3, 1, at(x, over), to_right)
        send(m, 3, 1, at(x, over), to_left)
        for side in (left, right):
            landed(m, 1, 2, at(side, below))
            send(m, 1, 1, at(side, below), to_above)
            landed(m, 1, 2, at(side, above))
            send(m, 2, 1, at(side, above), to_below)
        for side in (below, above):
            landed(m, 0, 1, at(left, side))
            landed(m, 3, 1, at(left, side))
            send(m, 0, 1, at(left, side), to_right)
            landed(m, 0, 1, at(right, side))
            landed(m, 3, 1, at(right, side))
            send(m, 3, 1, at(right, side), to_left)

    def fourth_round(m):
        landed(m, 1, 1, at(across, below))
        landed(m, 2, 1, at(across, below))
        send(m, 1, 1, at(across, below), to_above)
        landed(m, 1, 1, at(across, above))
        landed(m, 2, 1, at(across, above))
        send(m, 2, 1, at(across, above), to_below)
        landed(m, 0, 1, at(left, over))
        landed(m, 3, 1, at(left, over))
        send(m, 0, 1, at(left, over), to_right)
        landed(m, 0, 1, at(right, over))
        landed(m, 3, 1, at(right, over))
        send(m, 3, 1, at(right, over), to_left)

    def last_round(m):
        for side in (left, right):
            landed(m, 1, 1, at(side, over))
            landed(m, 2, 1, at(side, over))
        for side in (below, above):
            landed(m, 0, 1, at(across, side))
            landed(m, 3, 1, at(across, side))
        for q in range(QUARTERS):
            landed(m, q, 1, at(across, over))

    def matrix(m, q):
        return wall[m, q].reshape(-1, quarter)

    def project(m):
        @pl.loop(0, QUARTERS)
        def _(q):
            cols = pl.ds(pl.multiple_of(q * quarter, quarter), quarter)
            part = lax.dot_general(
                arrived[:, :, cols].reshape(count, quarter), matrix(m, q), TURNED, preferred_element_type=jnp.float32
            )
            sums[m] = jnp.where(q == 0, part, sums[m] + part)

    first_round(0)
    first_round(1)
    key_copy.wait()
    value_copy.wait()
    kv_copies = []
    copy = pltpu.make_async_remote_copy(
        src_ref=window.at[DEPTH, core], dst_ref=window.at[0, core],
        send_sem=kv_out.at[0], recv_sem=kv_in.at[0],
        device_id=(dp, next_ctx, ex), device_id_type=MESH,
    )
    copy.start()
    kv_copies.append(copy)

    hidden_copy.wait()
    picks = slot_hits(routes[...]).reshape(count, -1).astype(jnp.bfloat16)
    rows = hidden_rows[...].astype(jnp.float32)
    scale = lax.rsqrt(jnp.mean(rows * rows, axis=-1, keepdims=True) + 1e-06)
    for q in range(QUARTERS):
        cols = pl.ds(q * quarter, quarter)
        normed = (hidden_rows[:, cols].astype(jnp.float32) * scale * gain[:, cols]).astype(jnp.bfloat16)
        block = jnp.dot(picks, normed, preferred_element_type=jnp.float32).astype(jnp.bfloat16)
        packed[:, :, cols] = block.reshape(16, CAP, quarter)
    own_rows = pltpu.make_async_copy(packed.at[ex], arrived.at[ex], local_sem.at[16])
    own_rows.start()
    route_copies = []
    far_first = (8, 7, 9, 6, 10, 5, 11, 4, 12, 3, 13, 2, 14, 1, 15)
    for step in far_first:
        peer = lax.rem(ex + step, 16)
        copy = pltpu.make_async_remote_copy(
            src_ref=packed.at[peer], dst_ref=arrived.at[ex],
            send_sem=route_out.at[step - 1], recv_sem=route_in.at[ex],
            device_id=(dp, ctx, peer), device_id_type=MESH,
        )
        copy.start()
        route_copies.append(copy)

    second_round(0)
    first_round(2)
    second_round(1)
    third_round(0)
    second_round(2)

    pltpu.make_async_copy(window.at[0, core], window.at[0, core], kv_in.at[0]).wait()
    for step in range(1, DEPTH):
        wraps = (z + step) // DEPTH
        copy = pltpu.make_async_remote_copy(
            src_ref=window.at[DEPTH * (1 - wraps), core], dst_ref=window.at[DEPTH - step, core],
            send_sem=kv_out.at[step], recv_sem=kv_in.at[DEPTH - step],
            device_id=(dp, ctx, lax.rem(z + step, DEPTH) * 2 + core), device_id_type=MESH,
        )
        copy.start()
        kv_copies.append(copy)

    third_round(1)
    fourth_round(0)
    third_round(2)
    fourth_round(1)
    last_round(0)
    own_rows.wait()
    for step in range(1, 16):
        peer = lax.rem(ex + step, 16)
        pltpu.make_async_copy(arrived.at[peer], arrived.at[peer], route_in.at[peer]).wait()
    project(0)
    fourth_round(2)
    last_round(1)
    project(1)
    g = sums[0]
    active[...] = (g / (1.0 + jnp.exp(-g)) * sums[1]).astype(jnp.bfloat16)
    last_round(2)

    back_copies = []
    for q in range(QUARTERS):
        block = jnp.dot(active[...], matrix(2, q), preferred_element_type=jnp.float32)
        results[q] = block.astype(jnp.bfloat16).reshape(16, CAP, quarter)
        own = pltpu.make_async_copy(results.at[q, ex], returned.at[q, ex], back_own.at[q])
        own.start()
        local.append(own)
        for step in far_first:
            peer = lax.rem(ex + step, 16)
            copy = pltpu.make_async_remote_copy(
                src_ref=results.at[q, peer], dst_ref=returned.at[q, ex],
                send_sem=back_out.at[q, step - 1], recv_sem=back_in.at[q, ex],
                device_id=(dp, ctx, peer), device_id_type=MESH,
            )
            copy.start()
            back_copies.append(copy)

    for slot in range(1, DEPTH):
        pltpu.make_async_copy(window.at[slot, core], window.at[slot, core], kv_in.at[slot]).wait()
    share = pltpu.make_async_remote_copy(
        src_ref=window.at[:, core], dst_ref=window.at[:, core],
        send_sem=kv_out.at[DEPTH], recv_sem=kv_in.at[DEPTH],
        device_id=(dp, ctx, sibling), device_id_type=MESH,
    )
    share.start()
    attention_bias(lengths, query_rows.shape[0], bias)
    query_copy.wait()
    pltpu.make_async_copy(window.at[:, 1 - core], window.at[:, 1 - core], kv_in.at[DEPTH]).wait()

    @pl.loop(0, QUERY_HEADS // HEADS_AT_ONCE)
    def _(i):
        attend(i, query_rows, window, bias, context)

    ids = lax.broadcasted_iota(jnp.int32, (16, routes.shape[1]), 0)
    weight = jnp.where(ids == routes[0:1, :], gates[0:1, :], 0.0)
    weight = weight + jnp.where(ids == routes[1:2, :], gates[1:2, :], 0.0)
    spread = (slot_hits(routes[...]) * weight[:, None, :]).reshape(count, -1)
    high = spread.astype(jnp.bfloat16)
    low = (spread - high.astype(jnp.float32)).astype(jnp.bfloat16)
    by_slot = (((0,), (0,)), ((), ()))
    for q in range(QUARTERS):
        local[3 * QUARTERS + q].wait()
        for step in range(1, 16):
            peer = lax.rem(ex + step, 16)
            pltpu.make_async_copy(returned.at[q, peer], returned.at[q, peer], back_in.at[q, peer]).wait()
        block = returned[q].reshape(count, quarter)
        total = lax.dot_general(high, block, by_slot, preferred_element_type=jnp.float32)
        total = total + lax.dot_general(low, block, by_slot, preferred_element_type=jnp.float32)
        mixture[:, q * quarter:(q + 1) * quarter] = total.astype(mixture.dtype)

    share.wait_send()
    for copy in kv_copies + route_copies + sent + back_copies:
        copy.wait_send()


def shards(queries, keys, values, lengths, hidden, norm_gain, routes, gates, w_gate, w_up, w_down):
    tokens, width = hidden.shape
    turned = [jnp.swapaxes(w[0], 0, 1) for w in (w_gate, w_up, w_down)]
    piece, quarter = turned[0].shape[0], width // QUARTERS
    units, count = piece * SIDE * SIDE, 16 * CAP
    far, vmem = pl.BlockSpec(memory_space=pltpu.HBM), pl.BlockSpec(memory_space=pltpu.VMEM)
    bf16, f32, dma = jnp.bfloat16, jnp.float32, pltpu.SemaphoreType.DMA
    out = jax.ShapeDtypeStruct((tokens, width), bf16)
    return pl.pallas_call(
        kernel,
        out_shape=(out, out),
        in_specs=[far] * 7 + [vmem] * 3 + [pl.BlockSpec(memory_space=pltpu.SMEM)],
        out_specs=[vmem] * 2,
        scratch_shapes=[
            pltpu.VMEM((3, QUARTERS, SIDE * SIDE, piece, quarter), bf16),
            pltpu.VMEM((DEPTH + 1, 2, tokens, 2 * keys.shape[1]), bf16),
            pltpu.VMEM((tokens, width), bf16),
            pltpu.VMEM((tokens, width), bf16),
            pltpu.VMEM((16, CAP, width), bf16),
            pltpu.VMEM((16, CAP, width), bf16),
            pltpu.VMEM((QUARTERS, 16, CAP, quarter), bf16),
            pltpu.VMEM((QUARTERS, 16, CAP, quarter), bf16),
            pltpu.VMEM((2, count, units), f32),
            pltpu.VMEM((count, units), bf16),
            pltpu.VMEM((tokens, (DEPTH + 1) * 2 * tokens), f32),
            dma((17,)), dma((3, 40)), dma((3, 16, 4)), dma((15,)), dma((16,)), dma((9,)), dma((9,)),
            dma((QUARTERS, 15)), dma((QUARTERS, 16)), dma((QUARTERS,)),
        ],
        compiler_params=pltpu.CompilerParams(
            collective_id=0, has_side_effects=True, vmem_limit_bytes=60 * 1024 * 1024
        ),
        cost_estimate=pl.CostEstimate(flops=20 * 10**9, bytes_accessed=10 * 10**6, transcendentals=10**7),
        name="whole_block",
    )(*turned, queries, keys, values, hidden, norm_gain[None, :], routes.T, gates.T, lengths)


def solution(mesh):
    whole = P(("dp", "ctx", "exp"), None)
    weights = P("exp", None, ("dp", "ctx"))
    return jax.shard_map(
        shards,
        mesh=mesh,
        in_specs=(whole, whole, whole, P("dp", None), whole, P(), whole, whole, weights, weights, weights),
        out_specs=(whole, whole),
        check_vma=False,
    )
```

```python
import math

import jax
import jax.numpy as jnp
from jax import lax
from jax.experimental import pallas as pl
from jax.experimental.pallas import tpu as pltpu
from jax.sharding import PartitionSpec as P

MESH = pl.DeviceIdType.MESH
HEAD_WIDTH = 128
QUERY_HEADS = 32
KEY_HEADS = 2
SIDE = 4
DEPTH = 8
QUARTERS = 4
CAP = 24
HEADS_AT_ONCE = 4
TURNED = (((1,), (1,)), ((), ()))


def place():
    dp, ctx, ex = lax.axis_index("dp"), lax.axis_index("ctx"), lax.axis_index("exp")
    return (ctx % 2) * 2 + dp, ctx // 2, ex // 2, ex % 2


def device_at(x, y, ex):
    return (x % 2, y * 2 + x // 2, ex)


def slot_hits(routes):
    experts, tokens = 16, routes.shape[1]
    ids = lax.broadcasted_iota(jnp.int32, (experts, tokens), 0)
    hits = ((ids == routes[0:1, :]) | (ids == routes[1:2, :])).astype(jnp.float32)
    earlier = (
        lax.broadcasted_iota(jnp.int32, (tokens, tokens), 0)
        < lax.broadcasted_iota(jnp.int32, (tokens, tokens), 1)
    ).astype(jnp.bfloat16)
    ranks = jnp.dot(hits.astype(jnp.bfloat16), earlier, preferred_element_type=jnp.float32)
    ranks = jnp.where(hits > 0, ranks, -1.0).astype(jnp.int32)
    wanted = lax.broadcasted_iota(jnp.int32, (experts, CAP, tokens), 1)
    return (ranks[:, None, :] == wanted).astype(jnp.float32)


def attention_bias(lengths, tokens, bias):
    ctx, ex = lax.axis_index("ctx"), lax.axis_index("exp")
    query_pos = (ctx * 16 + ex) * tokens + lax.broadcasted_iota(jnp.int32, (tokens, 1), 0)
    begin = jnp.zeros_like(query_pos)
    bound = jnp.int32(0)
    for r in range(lengths.shape[1]):
        bound = bound + lengths[0, r]
        begin = jnp.where(query_pos >= bound, bound, begin)
    first = (ctx * 16 + (ex // 2) * 2 - 16) * tokens
    step = 256
    for c in range(bias.shape[1] // step):
        key_pos = first + c * step + lax.broadcasted_iota(jnp.int32, (tokens, step), 1)
        seen = (key_pos <= query_pos) & (key_pos >= begin)
        bias[:, c * step:(c + 1) * step] = jnp.where(seen, 0.0, -1e30)


def attend(i, queries, window, bias, out):
    tokens, keys = bias.shape
    columns = HEADS_AT_ONCE * HEAD_WIDTH
    place_of = pl.multiple_of(i * columns, columns)
    group = i // (QUERY_HEADS // KEY_HEADS // HEADS_AT_ONCE)
    key_col = pl.multiple_of(group * HEAD_WIDTH, HEAD_WIDTH)
    value_col = pl.multiple_of((KEY_HEADS + group) * HEAD_WIDTH, HEAD_WIDTH)
    key_rows = window[:, :, :, pl.ds(key_col, HEAD_WIDTH)].reshape(keys, HEAD_WIDTH)
    value_rows = window[:, :, :, pl.ds(value_col, HEAD_WIDTH)].reshape(keys, HEAD_WIDTH)
    block = queries[:, pl.ds(place_of, columns)]
    stacked = jnp.concatenate(
        [block[:, h * HEAD_WIDTH:(h + 1) * HEAD_WIDTH] for h in range(HEADS_AT_ONCE)], axis=0
    )
    scores = lax.dot_general(stacked, key_rows, TURNED, preferred_element_type=jnp.float32)
    scores = scores.reshape(HEADS_AT_ONCE, tokens, keys) + bias[...][None]
    top = jnp.max(scores, axis=-1, keepdims=True)
    probs = jnp.exp2((scores - top) * (math.log2(math.e) / math.sqrt(HEAD_WIDTH)))
    total = jnp.sum(probs, axis=-1, keepdims=True)
    summed = jnp.dot(
        probs.reshape(HEADS_AT_ONCE * tokens, keys).astype(jnp.bfloat16), value_rows,
        preferred_element_type=jnp.float32,
    ).reshape(HEADS_AT_ONCE, tokens, HEAD_WIDTH)
    result = (summed / total).astype(out.dtype)
    out[:, pl.ds(place_of, columns)] = jnp.concatenate([result[h] for h in range(HEADS_AT_ONCE)], axis=1)


def kernel(
    w_gate, w_up, w_down, queries, keys, values, hidden, gain, routes, gates, lengths,
    context, mixture,
    wall, window, hidden_rows, query_rows, packed, arrived, results, returned, sums, active, bias,
    local_sem, pass_sem, first_sem, out_sem, in_sem, route_out, route_in, kv_out, kv_in, back_out, back_in,
):
    x, y, z, core = place()
    dp, ctx, ex = lax.axis_index("dp"), lax.axis_index("ctx"), lax.axis_index("exp")
    group, partner = x // 2, SIDE - 1 - x
    native = core == group
    beside = x + 1 - 2 * (x % 2)
    above, below, over = lax.rem(y + 1, SIDE), lax.rem(y + SIDE - 1, SIDE), lax.rem(y + 2, SIDE)
    to_beside, to_above, to_below = device_at(beside, y, ex), device_at(x, above, ex), device_at(x, below, ex)
    sibling = z * 2 + 1 - core
    to_sibling = (dp, ctx, sibling)
    prior_ctx, next_ctx = lax.rem(ctx + 7, 8), lax.rem(ctx + 1, 8)
    expert = z * 2 + group
    rows_x = jnp.where(native, x, partner)
    quarter = wall.shape[-1]
    count = arrived.shape[1] * arrived.shape[2]

    def at(chip_x, chip_y):
        return chip_y * SIDE + jnp.where(native, chip_x, SIDE - 1 - chip_x)

    def shard_copies(remote):
        copies = []
        for m, source in enumerate((w_gate, w_up, w_down)):
            for q in range(QUARTERS):
                part = source.at[:, pl.ds(q * quarter, quarter)]
                home, arrival = wall.at[m, q, y * SIDE + x], in_sem.at[m, y * SIDE + x, q]
                if remote:
                    copies.append(pltpu.make_async_remote_copy(
                        src_ref=part, dst_ref=home, send_sem=pass_sem.at[m, q], recv_sem=arrival,
                        device_id=device_at(partner, y, sibling), device_id_type=MESH,
                    ))
                else:
                    copies.append(pltpu.make_async_copy(part, home, arrival))
        return copies

    @pl.when(native)
    def _():
        for copy in shard_copies(False):
            copy.start()

    width = keys.shape[1]
    key_copy = pltpu.make_async_copy(keys, window.at[DEPTH, core, :, pl.ds(0, width)], local_sem.at[0])
    value_copy = pltpu.make_async_copy(values, window.at[DEPTH, core, :, pl.ds(width, width)], local_sem.at[1])
    hidden_copy = pltpu.make_async_copy(hidden, hidden_rows, local_sem.at[2])
    query_copy = pltpu.make_async_copy(queries, query_rows, local_sem.at[3])
    for copy in (hidden_copy, key_copy, value_copy, query_copy):
        copy.start()

    barrier = pltpu.get_barrier_semaphore()
    for neighbour in (to_beside, to_above, to_below, (dp, prior_ctx, ex)):
        pl.semaphore_signal(barrier, inc=1, device_id=neighbour, device_id_type=MESH)
    for step in range(16):
        other = lax.rem(ex + step, 16)
        if step:
            pl.semaphore_signal(barrier, inc=1, device_id=(dp, ctx, other), device_id_type=MESH)
        pl.semaphore_signal(barrier, inc=1, device_id=device_at(partner, y, other), device_id_type=MESH)
    pl.semaphore_wait(barrier, 4 + 15 + 16)

    @pl.when(jnp.logical_not(native))
    def _():
        for copy in shard_copies(True):
            copy.start()

    sent = []
    counts = [0, 0, 0]

    def send(m, first, number, shard, target):
        part = wall.at[m, pl.ds(first, number), shard]
        copy = pltpu.make_async_remote_copy(
            src_ref=part, dst_ref=part,
            send_sem=out_sem.at[m, counts[m]], recv_sem=in_sem.at[m, shard, first],
            device_id=target, device_id_type=MESH,
        )
        counts[m] += 1
        copy.start()
        sent.append(copy)

    def landed(m, first, number, shard):
        part = wall.at[m, pl.ds(first, number), shard]
        pltpu.make_async_copy(part, part, in_sem.at[m, shard, first]).wait()

    def first_copies(m):
        part = wall.at[m, :, at(x, y)]
        return [
            pltpu.make_async_remote_copy(
                src_ref=part, dst_ref=part, send_sem=first_sem.at[m, i], recv_sem=in_sem.at[m, at(x, y), 0],
                device_id=target, device_id_type=MESH,
            )
            for i, target in enumerate((to_beside, to_above, to_below, to_sibling))
        ]

    def share_shard(m, shard):
        send(m, 0, 4, shard, to_sibling)

    def first_round(m):
        for q in range(QUARTERS):
            landed(m, q, 1, at(x, y))
        for copy in first_copies(m):
            copy.start()

    def second_round(m):
        landed(m, 0, 4, at(beside, y))
        send(m, 1, 2, at(beside, y), to_above)
        send(m, 1, 2, at(beside, y), to_below)
        landed(m, 0, 4, at(x, below))
        send(m, 0, 2, at(x, below), to_above)
        send(m, 0, 1, at(x, below), to_beside)
        send(m, 3, 1, at(x, below), to_beside)
        landed(m, 0, 4, at(x, above))
        send(m, 2, 2, at(x, above), to_below)
        send(m, 0, 1, at(x, above), to_beside)
        send(m, 3, 1, at(x, above), to_beside)
        for shard in (at(beside, y), at(x, below), at(x, above)):
            share_shard(m, shard)

    def third_round(m):
        landed(m, 0, 2, at(x, over))
        send(m, 0, 1, at(x, over), to_beside)
        landed(m, 2, 2, at(x, over))
        send(m, 3, 1, at(x, over), to_beside)
        landed(m, 1, 2, at(beside, below))
        send(m, 1, 1, at(beside, below), to_above)
        landed(m, 1, 2, at(beside, above))
        send(m, 2, 1, at(beside, above), to_below)
        share_shard(m, at(x, over))
        for side in (below, above):
            landed(m, 0, 1, at(beside, side))
            landed(m, 3, 1, at(beside, side))
            share_shard(m, at(beside, side))

    def fourth_round(m):
        for q in range(QUARTERS):
            landed(m, q, 1, at(beside, over))
        share_shard(m, at(beside, over))

    def last_round(m):
        for row in range(SIDE):
            for chip in (x, beside):
                landed(m, 0, 4, row * SIDE + jnp.where(native, SIDE - 1 - chip, chip))

    def matrix(m, q):
        return wall[m, q].reshape(-1, quarter)

    def project(m):
        @pl.loop(0, QUARTERS)
        def _(q):
            part = lax.dot_general(
                arrived[q].reshape(count, quarter), matrix(m, q), TURNED, preferred_element_type=jnp.float32
            )
            sums[m] = jnp.where(q == 0, part, sums[m] + part)

    def route_copy(q, step, c):
        plane = lax.rem(z + step, DEPTH)
        wanted = plane * 2 + (group if c == 0 else 1 - group)
        return pltpu.make_async_remote_copy(
            src_ref=packed.at[q, wanted], dst_ref=arrived.at[q, ex],
            send_sem=route_out.at[q, 2 * step + c], recv_sem=route_in.at[q, ex],
            device_id=device_at(x if c == 0 else partner, y, plane * 2 + group), device_id_type=MESH,
        )

    def back_copy(q, step, c):
        source = lax.rem(z + step, DEPTH) * 2 + (core if c == 0 else 1 - core)
        return pltpu.make_async_remote_copy(
            src_ref=results.at[q, source], dst_ref=returned.at[q, expert],
            send_sem=back_out.at[q, 2 * step + c], recv_sem=back_in.at[q, expert],
            device_id=device_at(rows_x, y, source), device_id_type=MESH,
        )

    far_first = (4, 3, 5, 2, 6, 1, 7, 0)

    def scatter(make, q, own):
        for step in far_first:
            for c in (0, 1):
                if step or c:
                    make(q, step, c).start()

        @pl.when(native)
        def _():
            own.start()

        @pl.when(jnp.logical_not(native))
        def _():
            make(q, 0, 0).start()

    def scattered(make, q):
        for step in far_first:
            for c in (0, 1):
                if step or c:
                    make(q, step, c).wait_send()

        @pl.when(jnp.logical_not(native))
        def _():
            make(q, 0, 0).wait_send()

    @pl.when(native)
    def _():
        first_round(0)
        first_round(1)

    key_copy.wait()
    value_copy.wait()
    kv_copies = []
    copy = pltpu.make_async_remote_copy(
        src_ref=window.at[DEPTH, core], dst_ref=window.at[0, core],
        send_sem=kv_out.at[0], recv_sem=kv_in.at[0],
        device_id=(dp, next_ctx, ex), device_id_type=MESH,
    )
    copy.start()
    kv_copies.append(copy)

    hidden_copy.wait()
    picks = slot_hits(routes[...]).reshape(count, -1).astype(jnp.bfloat16)
    rows = hidden_rows[...].astype(jnp.float32)
    scale = lax.rsqrt(jnp.mean(rows * rows, axis=-1, keepdims=True) + 1e-06)
    for q in range(QUARTERS):
        cols = pl.ds(q * quarter, quarter)
        normed = (hidden_rows[:, cols].astype(jnp.float32) * scale * gain[:, cols]).astype(jnp.bfloat16)
        block = jnp.dot(picks, normed, preferred_element_type=jnp.float32).astype(jnp.bfloat16)
        packed[q] = block.reshape(16, CAP, quarter)
        scatter(route_copy, q, pltpu.make_async_copy(packed.at[q, ex], arrived.at[q, ex], route_in.at[q, ex]))

    @pl.when(jnp.logical_not(native))
    def _():
        first_round(0)
        first_round(1)

    second_round(0)
    first_round(2)
    second_round(1)
    third_round(0)
    second_round(2)
    third_round(1)
    fourth_round(0)
    third_round(2)
    fourth_round(1)
    last_round(0)
    fourth_round(2)
    for q in range(QUARTERS):
        scattered(route_copy, q)

    pltpu.make_async_copy(window.at[0, core], window.at[0, core], kv_in.at[0]).wait()
    for step in range(1, DEPTH):
        wraps = (z + step) // DEPTH
        copy = pltpu.make_async_remote_copy(
            src_ref=window.at[DEPTH * (1 - wraps), core], dst_ref=window.at[DEPTH - step, core],
            send_sem=kv_out.at[step], recv_sem=kv_in.at[DEPTH - step],
            device_id=(dp, ctx, lax.rem(z + step, DEPTH) * 2 + core), device_id_type=MESH,
        )
        copy.start()
        kv_copies.append(copy)

    for q in range(QUARTERS):
        for source in range(16):
            pltpu.make_async_copy(arrived.at[q, source], arrived.at[q, source], route_in.at[q, source]).wait()
    project(0)
    last_round(1)
    project(1)
    g = sums[0]
    active[...] = (g / (1.0 + jnp.exp(-g)) * sums[1]).astype(jnp.bfloat16)
    last_round(2)

    for q in range(QUARTERS):
        block = jnp.dot(active[...], matrix(2, q), preferred_element_type=jnp.float32)
        results[q] = block.astype(jnp.bfloat16).reshape(16, CAP, quarter)
        scatter(back_copy, q, pltpu.make_async_copy(results.at[q, ex], returned.at[q, ex], back_in.at[q, ex]))

    for slot in range(1, DEPTH):
        pltpu.make_async_copy(window.at[slot, core], window.at[slot, core], kv_in.at[slot]).wait()
    share = pltpu.make_async_remote_copy(
        src_ref=window.at[:, core], dst_ref=window.at[:, core],
        send_sem=kv_out.at[DEPTH], recv_sem=kv_in.at[DEPTH],
        device_id=to_sibling, device_id_type=MESH,
    )
    share.start()
    attention_bias(lengths, query_rows.shape[0], bias)
    query_copy.wait()
    pltpu.make_async_copy(window.at[:, 1 - core], window.at[:, 1 - core], kv_in.at[DEPTH]).wait()

    @pl.loop(0, QUERY_HEADS // HEADS_AT_ONCE)
    def _(i):
        attend(i, query_rows, window, bias, context)

    ids = lax.broadcasted_iota(jnp.int32, (16, routes.shape[1]), 0)
    weight = jnp.where(ids == routes[0:1, :], gates[0:1, :], 0.0)
    weight = weight + jnp.where(ids == routes[1:2, :], gates[1:2, :], 0.0)
    spread = (slot_hits(routes[...]) * weight[:, None, :]).reshape(count, -1)
    high = spread.astype(jnp.bfloat16)
    low = (spread - high.astype(jnp.float32)).astype(jnp.bfloat16)
    by_slot = (((0,), (0,)), ((), ()))
    for q in range(QUARTERS):
        for e in range(16):
            pltpu.make_async_copy(returned.at[q, e], returned.at[q, e], back_in.at[q, e]).wait()
        block = returned[q].reshape(count, quarter)
        total = lax.dot_general(high, block, by_slot, preferred_element_type=jnp.float32)
        total = total + lax.dot_general(low, block, by_slot, preferred_element_type=jnp.float32)
        mixture[:, q * quarter:(q + 1) * quarter] = total.astype(mixture.dtype)

    share.wait_send()
    for m in range(3):
        for copy in first_copies(m):
            copy.wait_send()
    for copy in kv_copies + sent:
        copy.wait_send()
    for q in range(QUARTERS):
        scattered(back_copy, q)

    @pl.when(jnp.logical_not(native))
    def _():
        for copy in shard_copies(True):
            copy.wait_send()


def shards(queries, keys, values, lengths, hidden, norm_gain, routes, gates, w_gate, w_up, w_down):
    tokens, width = hidden.shape
    turned = [jnp.swapaxes(w[0], 0, 1) for w in (w_gate, w_up, w_down)]
    piece, quarter = turned[0].shape[0], width // QUARTERS
    units, count = piece * SIDE * SIDE, 16 * CAP
    far, vmem = pl.BlockSpec(memory_space=pltpu.HBM), pl.BlockSpec(memory_space=pltpu.VMEM)
    bf16, f32, dma = jnp.bfloat16, jnp.float32, pltpu.SemaphoreType.DMA
    out = jax.ShapeDtypeStruct((tokens, width), bf16)
    return pl.pallas_call(
        kernel,
        out_shape=(out, out),
        in_specs=[far] * 7 + [vmem] * 3 + [pl.BlockSpec(memory_space=pltpu.SMEM)],
        out_specs=[vmem] * 2,
        scratch_shapes=[
            pltpu.VMEM((3, QUARTERS, SIDE * SIDE, piece, quarter), bf16),
            pltpu.VMEM((DEPTH + 1, 2, tokens, 2 * keys.shape[1]), bf16),
            pltpu.VMEM((tokens, width), bf16),
            pltpu.VMEM((tokens, width), bf16),
            pltpu.VMEM((QUARTERS, 16, CAP, quarter), bf16),
            pltpu.VMEM((QUARTERS, 16, CAP, quarter), bf16),
            pltpu.VMEM((QUARTERS, 16, CAP, quarter), bf16),
            pltpu.VMEM((QUARTERS, 16, CAP, quarter), bf16),
            pltpu.VMEM((2, count, units), f32),
            pltpu.VMEM((count, units), bf16),
            pltpu.VMEM((tokens, (DEPTH + 1) * 2 * tokens), f32),
            dma((4,)), dma((3, QUARTERS)), dma((3, 4)), dma((3, 20)), dma((3, 16, QUARTERS)), dma((QUARTERS, 16)), dma((QUARTERS, 16)),
            dma((9,)), dma((9,)), dma((QUARTERS, 16)), dma((QUARTERS, 16)),
        ],
        compiler_params=pltpu.CompilerParams(
            collective_id=0, has_side_effects=True, vmem_limit_bytes=60 * 1024 * 1024
        ),
        cost_estimate=pl.CostEstimate(flops=20 * 10**9, bytes_accessed=10 * 10**6, transcendentals=10**7),
        name="whole_block",
    )(*turned, queries, keys, values, hidden, norm_gain[None, :], routes.T, gates.T, lengths)


def solution(mesh):
    whole = P(("dp", "ctx", "exp"), None)
    weights = P("exp", None, ("dp", "ctx"))
    return jax.shard_map(
        shards,
        mesh=mesh,
        in_specs=(whole, whole, whole, P("dp", None), whole, P(), whole, whole, weights, weights, weights),
        out_specs=(whole, whole),
        check_vma=False,
    )
```

```python
import math

import jax
import jax.numpy as jnp
from jax import lax
from jax.experimental import pallas as pl
from jax.experimental.pallas import tpu as pltpu
from jax.sharding import PartitionSpec as P

MESH = pl.DeviceIdType.MESH
HEAD_WIDTH = 128
QUERY_HEADS = 32
KEY_HEADS = 2
SIDE = 4
DEPTH = 8
QUARTERS = 4
CAP = 24
HEADS_AT_ONCE = 4
TURNED = (((1,), (1,)), ((), ()))


def place():
    dp, ctx, ex = lax.axis_index("dp"), lax.axis_index("ctx"), lax.axis_index("exp")
    return (ctx % 2) * 2 + dp, ctx // 2, ex // 2, ex % 2


def device_at(x, y, ex):
    return (x % 2, y * 2 + x // 2, ex)


def slot_hits(routes):
    experts, tokens = 16, routes.shape[1]
    ids = lax.broadcasted_iota(jnp.int32, (experts, tokens), 0)
    hits = ((ids == routes[0:1, :]) | (ids == routes[1:2, :])).astype(jnp.float32)
    earlier = (
        lax.broadcasted_iota(jnp.int32, (tokens, tokens), 0)
        < lax.broadcasted_iota(jnp.int32, (tokens, tokens), 1)
    ).astype(jnp.bfloat16)
    ranks = jnp.dot(hits.astype(jnp.bfloat16), earlier, preferred_element_type=jnp.float32)
    ranks = jnp.where(hits > 0, ranks, -1.0).astype(jnp.int32)
    wanted = lax.broadcasted_iota(jnp.int32, (experts, CAP, tokens), 1)
    return (ranks[:, None, :] == wanted).astype(jnp.float32)


def attention_bias(lengths, tokens, bias):
    ctx, ex = lax.axis_index("ctx"), lax.axis_index("exp")
    query_pos = (ctx * 16 + ex) * tokens + lax.broadcasted_iota(jnp.int32, (tokens, 1), 0)
    begin = jnp.zeros_like(query_pos)
    bound = jnp.int32(0)
    for r in range(lengths.shape[1]):
        bound = bound + lengths[0, r]
        begin = jnp.where(query_pos >= bound, bound, begin)
    first = (ctx * 16 + (ex // 2) * 2 - 16) * tokens
    step = 256
    for c in range(bias.shape[1] // step):
        key_pos = first + c * step + lax.broadcasted_iota(jnp.int32, (tokens, step), 1)
        seen = (key_pos <= query_pos) & (key_pos >= begin)
        bias[:, c * step:(c + 1) * step] = jnp.where(seen, 0.0, -1e30)


def attend(i, queries, window, bias, out):
    tokens, keys = bias.shape
    columns = HEADS_AT_ONCE * HEAD_WIDTH
    place_of = pl.multiple_of(i * columns, columns)
    group = i // (QUERY_HEADS // KEY_HEADS // HEADS_AT_ONCE)
    key_col = pl.multiple_of(group * HEAD_WIDTH, HEAD_WIDTH)
    value_col = pl.multiple_of((KEY_HEADS + group) * HEAD_WIDTH, HEAD_WIDTH)
    key_rows = window[:, :, :, pl.ds(key_col, HEAD_WIDTH)].reshape(keys, HEAD_WIDTH)
    value_rows = window[:, :, :, pl.ds(value_col, HEAD_WIDTH)].reshape(keys, HEAD_WIDTH)
    block = queries[:, pl.ds(place_of, columns)]
    stacked = jnp.concatenate(
        [block[:, h * HEAD_WIDTH:(h + 1) * HEAD_WIDTH] for h in range(HEADS_AT_ONCE)], axis=0
    )
    scores = lax.dot_general(stacked, key_rows, TURNED, preferred_element_type=jnp.float32)
    scores = scores.reshape(HEADS_AT_ONCE, tokens, keys) + bias[...][None]
    top = jnp.max(scores, axis=-1, keepdims=True)
    probs = jnp.exp2((scores - top) * (math.log2(math.e) / math.sqrt(HEAD_WIDTH)))
    total = jnp.sum(probs, axis=-1, keepdims=True)
    summed = jnp.dot(
        probs.reshape(HEADS_AT_ONCE * tokens, keys).astype(jnp.bfloat16), value_rows,
        preferred_element_type=jnp.float32,
    ).reshape(HEADS_AT_ONCE, tokens, HEAD_WIDTH)
    result = (summed / total).astype(out.dtype)
    out[:, pl.ds(place_of, columns)] = jnp.concatenate([result[h] for h in range(HEADS_AT_ONCE)], axis=1)


def kernel(
    w_gate, w_up, w_down, queries, keys, values, hidden, gain, routes, gates, lengths,
    context, mixture,
    wall, window, hidden_rows, query_rows, context_rows, mixture_rows, packed, arrived, results, returned, sums, active, bias,
    local_sem, pass_out, own_in, out_sem, in_sem, share_in, route_out, route_in, kv_out, kv_in, back_out, back_in,
):
    x, y, z, core = place()
    dp, ctx, ex = lax.axis_index("dp"), lax.axis_index("ctx"), lax.axis_index("exp")
    group, partner = x // 2, SIDE - 1 - x
    native = core == group
    beside = x + 1 - 2 * (x % 2)
    above, below, over = lax.rem(y + 1, SIDE), lax.rem(y + SIDE - 1, SIDE), lax.rem(y + 2, SIDE)
    to_beside, to_above, to_below = device_at(beside, y, ex), device_at(x, above, ex), device_at(x, below, ex)
    sibling = z * 2 + 1 - core
    to_sibling = (dp, ctx, sibling)
    prior_ctx, next_ctx = lax.rem(ctx + 7, 8), lax.rem(ctx + 1, 8)
    expert = z * 2 + group
    rows_x = jnp.where(native, x, partner)
    quarter = wall.shape[-1]
    count = arrived.shape[1] * arrived.shape[2]

    def at(chip_x, chip_y):
        return chip_y * SIDE + jnp.where(native, chip_x, SIDE - 1 - chip_x)

    def shard_copies(remote):
        copies = []
        for m, source in enumerate((w_gate, w_up, w_down)):
            for q in range(QUARTERS):
                part = source.at[:, pl.ds(q * quarter, quarter)]
                home, arrival = wall.at[m, q, y * SIDE + x], own_in.at[m]
                if remote:
                    copies.append(pltpu.make_async_remote_copy(
                        src_ref=part, dst_ref=home, send_sem=pass_out, recv_sem=arrival,
                        device_id=device_at(partner, y, sibling), device_id_type=MESH,
                    ))
                else:
                    copies.append(pltpu.make_async_copy(part, home, arrival))
        return copies

    @pl.when(native)
    def _():
        for copy in shard_copies(False):
            copy.start()

    width = keys.shape[1]
    key_copy = pltpu.make_async_copy(keys, window.at[DEPTH, core, :, pl.ds(0, width)], local_sem.at[0])
    value_copy = pltpu.make_async_copy(values, window.at[DEPTH, core, :, pl.ds(width, width)], local_sem.at[1])
    hidden_copy = pltpu.make_async_copy(hidden, hidden_rows, local_sem.at[2])
    query_copy = pltpu.make_async_copy(queries, query_rows, local_sem.at[3])
    for copy in (hidden_copy, key_copy, value_copy, query_copy):
        copy.start()

    barrier = pltpu.get_barrier_semaphore()
    for neighbour in (to_beside, to_above, to_below, (dp, prior_ctx, ex)):
        pl.semaphore_signal(barrier, inc=1, device_id=neighbour, device_id_type=MESH)
    for step in range(16):
        other = lax.rem(ex + step, 16)
        if step:
            pl.semaphore_signal(barrier, inc=1, device_id=(dp, ctx, other), device_id_type=MESH)
        pl.semaphore_signal(barrier, inc=1, device_id=device_at(partner, y, other), device_id_type=MESH)

    hidden_copy.wait()
    picks = slot_hits(routes[...]).reshape(count, -1).astype(jnp.bfloat16)
    rows = hidden_rows[...].astype(jnp.float32)
    scale = lax.rsqrt(jnp.mean(rows * rows, axis=-1, keepdims=True) + 1e-06)
    for q in range(QUARTERS):
        cols = pl.ds(q * quarter, quarter)
        normed = (hidden_rows[:, cols].astype(jnp.float32) * scale * gain[:, cols]).astype(jnp.bfloat16)
        block = jnp.dot(picks, normed, preferred_element_type=jnp.float32).astype(jnp.bfloat16)
        packed[q] = block.reshape(16, CAP, quarter)
    key_copy.wait()
    value_copy.wait()
    pl.semaphore_wait(barrier, 4 + 15 + 16)

    @pl.when(jnp.logical_not(native))
    def _():
        for copy in shard_copies(True):
            copy.start()

    def send(m, first, number, shard, target, arrival):
        part = wall.at[m, pl.ds(first, number), shard]
        pltpu.make_async_remote_copy(
            src_ref=part, dst_ref=part, send_sem=out_sem.at[m], recv_sem=arrival,
            device_id=target, device_id_type=MESH,
        ).start()

    def landed(m, first, number, shard, index):
        part = wall.at[m, pl.ds(first, number), shard]
        pltpu.make_async_copy(part, part, in_sem.at[m, index]).wait()

    def wait_for(part, semaphore):
        pltpu.make_async_copy(part, part, semaphore).wait()

    def share_shard(m, shard):
        send(m, 0, 4, shard, to_sibling, share_in.at[m])

    def first_round(m):
        wait_for(wall.at[m, :, at(x, y)], own_in.at[m])
        for i, target in enumerate((to_beside, to_above, to_below)):
            send(m, 0, 4, at(x, y), target, in_sem.at[m, i])
        share_shard(m, at(x, y))

    def second_round(m):
        landed(m, 0, 4, at(beside, y), 0)
        send(m, 1, 2, at(beside, y), to_above, in_sem.at[m, 5])
        send(m, 1, 2, at(beside, y), to_below, in_sem.at[m, 8])
        landed(m, 0, 4, at(x, below), 1)
        send(m, 0, 2, at(x, below), to_above, in_sem.at[m, 3])
        send(m, 0, 1, at(x, below), to_beside, in_sem.at[m, 6])
        send(m, 3, 1, at(x, below), to_beside, in_sem.at[m, 7])
        landed(m, 0, 4, at(x, above), 2)
        send(m, 2, 2, at(x, above), to_below, in_sem.at[m, 4])
        send(m, 0, 1, at(x, above), to_beside, in_sem.at[m, 9])
        send(m, 3, 1, at(x, above), to_beside, in_sem.at[m, 10])
        for shard in (at(beside, y), at(x, below), at(x, above)):
            share_shard(m, shard)

    def third_round(m):
        landed(m, 0, 2, at(x, over), 3)
        send(m, 0, 1, at(x, over), to_beside, in_sem.at[m, 11])
        landed(m, 2, 2, at(x, over), 4)
        send(m, 3, 1, at(x, over), to_beside, in_sem.at[m, 14])
        landed(m, 1, 2, at(beside, below), 5)
        send(m, 1, 1, at(beside, below), to_above, in_sem.at[m, 12])
        landed(m, 1, 2, at(beside, above), 8)
        send(m, 2, 1, at(beside, above), to_below, in_sem.at[m, 13])
        share_shard(m, at(x, over))
        for side, index in ((below, 6), (above, 9)):
            landed(m, 0, 1, at(beside, side), index)
            landed(m, 3, 1, at(beside, side), index + 1)
            share_shard(m, at(beside, side))

    def fourth_round(m):
        for q in range(QUARTERS):
            landed(m, q, 1, at(beside, over), 11 + q)
        share_shard(m, at(beside, over))

    def last_round(m):
        wait_for(wall.at[m, :, pl.ds(0, 2 * SIDE)], share_in.at[m])

    def matrix(m, q):
        return wall[m, q].reshape(-1, quarter)

    def project(m):
        @pl.loop(0, QUARTERS)
        def _(q):
            part = lax.dot_general(
                arrived[q].reshape(count, quarter), matrix(m, q), TURNED, preferred_element_type=jnp.float32
            )
            sums[m] = jnp.where(q == 0, part, sums[m] + part)

    def route_copy(q, step, c):
        plane = lax.rem(z + step, DEPTH)
        wanted = plane * 2 + (group if c == 0 else 1 - group)
        return pltpu.make_async_remote_copy(
            src_ref=packed.at[q, wanted], dst_ref=arrived.at[q, ex],
            send_sem=route_out.at[q], recv_sem=route_in.at[q],
            device_id=device_at(x if c == 0 else partner, y, plane * 2 + group), device_id_type=MESH,
        )

    def back_copy(q, step, c):
        source = lax.rem(z + step, DEPTH) * 2 + (core if c == 0 else 1 - core)
        return pltpu.make_async_remote_copy(
            src_ref=results.at[q, source], dst_ref=returned.at[q, expert],
            send_sem=back_out.at[q], recv_sem=back_in.at[q],
            device_id=device_at(rows_x, y, source), device_id_type=MESH,
        )

    far_first = (4, 3, 5, 2, 6, 1, 7, 0)

    def scatter(make, q, own):
        for step in far_first:
            for c in (0, 1):
                if step or c:
                    make(q, step, c).start()

        @pl.when(native)
        def _():
            own.start()

        @pl.when(jnp.logical_not(native))
        def _():
            make(q, 0, 0).start()

    def scattered(block, semaphore):
        @pl.when(native)
        def _():
            wait_for(block.at[pl.ds(0, 15)], semaphore)

        @pl.when(jnp.logical_not(native))
        def _():
            wait_for(block, semaphore)

    def send_rows(q):
        scatter(route_copy, q, pltpu.make_async_copy(packed.at[q, ex], arrived.at[q, ex], route_in.at[q]))

    send_rows(0)

    @pl.when(native)
    def _():
        first_round(0)
        first_round(1)

    pltpu.make_async_remote_copy(
        src_ref=window.at[DEPTH, core], dst_ref=window.at[0, core],
        send_sem=kv_out.at[0], recv_sem=kv_in.at[0],
        device_id=(dp, next_ctx, ex), device_id_type=MESH,
    ).start()
    for q in range(1, QUARTERS):
        send_rows(q)

    @pl.when(jnp.logical_not(native))
    def _():
        first_round(0)
        first_round(1)

    second_round(0)
    first_round(2)
    second_round(1)
    third_round(0)
    second_round(2)
    third_round(1)
    fourth_round(0)
    third_round(2)
    fourth_round(1)
    last_round(0)
    fourth_round(2)
    for q in range(QUARTERS):
        scattered(packed.at[q], route_out.at[q])

    wait_for(window.at[0, core], kv_in.at[0])
    for step in range(1, DEPTH):
        wraps = (z + step) // DEPTH
        pltpu.make_async_remote_copy(
            src_ref=window.at[DEPTH * (1 - wraps), core], dst_ref=window.at[DEPTH - step, core],
            send_sem=kv_out.at[0], recv_sem=kv_in.at[1],
            device_id=(dp, ctx, lax.rem(z + step, DEPTH) * 2 + core), device_id_type=MESH,
        ).start()

    for q in range(QUARTERS):
        wait_for(arrived.at[q], route_in.at[q])
    project(0)
    last_round(1)
    project(1)
    g = sums[0]
    active[...] = (g / (1.0 + jnp.exp(-g)) * sums[1]).astype(jnp.bfloat16)
    last_round(2)

    for q in range(QUARTERS):
        block = jnp.dot(active[...], matrix(2, q), preferred_element_type=jnp.float32)
        results[q] = block.astype(jnp.bfloat16).reshape(16, CAP, quarter)
        scatter(back_copy, q, pltpu.make_async_copy(results.at[q, ex], returned.at[q, ex], back_in.at[q]))

    wait_for(window.at[pl.ds(1, DEPTH - 1), core], kv_in.at[1])
    share = pltpu.make_async_remote_copy(
        src_ref=window.at[:, core], dst_ref=window.at[:, core],
        send_sem=kv_out.at[1], recv_sem=kv_in.at[2],
        device_id=to_sibling, device_id_type=MESH,
    )
    share.start()
    attention_bias(lengths, query_rows.shape[0], bias)
    query_copy.wait()
    wait_for(window.at[:, 1 - core], kv_in.at[2])

    @pl.loop(0, QUERY_HEADS // HEADS_AT_ONCE)
    def _(i):
        attend(i, query_rows, window, bias, context_rows)

    context_copy = pltpu.make_async_copy(context_rows, context, local_sem.at[4])
    context_copy.start()
    ids = lax.broadcasted_iota(jnp.int32, (16, routes.shape[1]), 0)
    weight = jnp.where(ids == routes[0:1, :], gates[0:1, :], 0.0)
    weight = weight + jnp.where(ids == routes[1:2, :], gates[1:2, :], 0.0)
    spread = (slot_hits(routes[...]) * weight[:, None, :]).reshape(count, -1)
    high = spread.astype(jnp.bfloat16)
    low = (spread - high.astype(jnp.float32)).astype(jnp.bfloat16)
    by_slot = (((0,), (0,)), ((), ()))
    mixture_copies = []
    for q in range(QUARTERS):
        wait_for(returned.at[q], back_in.at[q])
        block = returned[q].reshape(count, quarter)
        total = lax.dot_general(high, block, by_slot, preferred_element_type=jnp.float32)
        total = total + lax.dot_general(low, block, by_slot, preferred_element_type=jnp.float32)
        cols = pl.ds(q * quarter, quarter)
        mixture_rows[:, cols] = total.astype(mixture.dtype)
        copy = pltpu.make_async_copy(mixture_rows.at[:, cols], mixture.at[:, cols], local_sem.at[5 + q])
        copy.start()
        mixture_copies.append(copy)

    share.wait_send()
    wait_for(window.at[pl.ds(0, DEPTH), core], kv_out.at[0])
    for m in range(3):
        wait_for(wall.at[m, :, pl.ds(0, 15)], out_sem.at[m])
    for q in range(QUARTERS):
        scattered(results.at[q], back_out.at[q])

    @pl.when(jnp.logical_not(native))
    def _():
        wait_for(wall.at[:, :, y * SIDE + x], pass_out)

    context_copy.wait()
    for copy in mixture_copies:
        copy.wait()


def shards(queries, keys, values, lengths, hidden, norm_gain, routes, gates, w_gate, w_up, w_down):
    tokens, width = hidden.shape
    turned = [jnp.swapaxes(w[0], 0, 1) for w in (w_gate, w_up, w_down)]
    piece, quarter = turned[0].shape[0], width // QUARTERS
    units, count = piece * SIDE * SIDE, 16 * CAP
    far, vmem = pl.BlockSpec(memory_space=pltpu.HBM), pl.BlockSpec(memory_space=pltpu.VMEM)
    bf16, f32, dma = jnp.bfloat16, jnp.float32, pltpu.SemaphoreType.DMA
    out = jax.ShapeDtypeStruct((tokens, width), bf16)
    return pl.pallas_call(
        kernel,
        out_shape=(out, out),
        in_specs=[far] * 7 + [vmem] * 3 + [pl.BlockSpec(memory_space=pltpu.SMEM)],
        out_specs=[far] * 2,
        scratch_shapes=[
            pltpu.VMEM((3, QUARTERS, SIDE * SIDE, piece, quarter), bf16),
            pltpu.VMEM((DEPTH + 1, 2, tokens, 2 * keys.shape[1]), bf16),
            pltpu.VMEM((tokens, width), bf16),
            pltpu.VMEM((tokens, width), bf16),
            pltpu.VMEM((tokens, width), bf16),
            pltpu.VMEM((tokens, width), bf16),
            pltpu.VMEM((QUARTERS, 16, CAP, quarter), bf16),
            pltpu.VMEM((QUARTERS, 16, CAP, quarter), bf16),
            pltpu.VMEM((QUARTERS, 16, CAP, quarter), bf16),
            pltpu.VMEM((QUARTERS, 16, CAP, quarter), bf16),
            pltpu.VMEM((2, count, units), f32),
            pltpu.VMEM((count, units), bf16),
            pltpu.VMEM((tokens, (DEPTH + 1) * 2 * tokens), f32),
            dma((9,)), dma(()), dma((3,)), dma((3,)), dma((3, 15)), dma((3,)), dma((QUARTERS,)), dma((QUARTERS,)),
            dma((2,)), dma((3,)), dma((QUARTERS,)), dma((QUARTERS,)),
        ],
        compiler_params=pltpu.CompilerParams(
            collective_id=0, has_side_effects=True, vmem_limit_bytes=60 * 1024 * 1024
        ),
        cost_estimate=pl.CostEstimate(flops=20 * 10**9, bytes_accessed=10 * 10**6, transcendentals=10**7),
        name="whole_block",
    )(*turned, queries, keys, values, hidden, norm_gain[None, :], routes.T, gates.T, lengths)


def solution(mesh):
    whole = P(("dp", "ctx", "exp"), None)
    weights = P("exp", None, ("dp", "ctx"))
    return jax.shard_map(
        shards,
        mesh=mesh,
        in_specs=(whole, whole, whole, P("dp", None), whole, P(), whole, whole, weights, weights, weights),
        out_specs=(whole, whole),
        check_vma=False,
    )
```

```python
import math

import jax
import jax.numpy as jnp
from jax import lax
from jax.experimental import pallas as pl
from jax.experimental.pallas import tpu as pltpu
from jax.sharding import PartitionSpec as P

MESH = pl.DeviceIdType.MESH
HEAD_WIDTH = 128
QUERY_HEADS = 32
KEY_HEADS = 2
SIDE = 4
DEPTH = 8
QUARTERS = 4
CAP = 24
HEADS_AT_ONCE = 4
TURNED = (((1,), (1,)), ((), ()))


def place():
    dp, ctx, ex = lax.axis_index("dp"), lax.axis_index("ctx"), lax.axis_index("exp")
    return (ctx % 2) * 2 + dp, ctx // 2, ex // 2, ex % 2


def device_at(x, y, ex):
    return (x % 2, y * 2 + x // 2, ex)


def slot_hits(routes):
    experts, tokens = 16, routes.shape[1]
    ids = lax.broadcasted_iota(jnp.int32, (experts, tokens), 0)
    hits = ((ids == routes[0:1, :]) | (ids == routes[1:2, :])).astype(jnp.float32)
    earlier = (
        lax.broadcasted_iota(jnp.int32, (tokens, tokens), 0)
        < lax.broadcasted_iota(jnp.int32, (tokens, tokens), 1)
    ).astype(jnp.bfloat16)
    ranks = jnp.dot(hits.astype(jnp.bfloat16), earlier, preferred_element_type=jnp.float32)
    ranks = jnp.where(hits > 0, ranks, -1.0).astype(jnp.int32)
    wanted = lax.broadcasted_iota(jnp.int32, (experts, CAP, tokens), 1)
    return (ranks[:, None, :] == wanted).astype(jnp.float32)


def attention_bias(lengths, tokens, bias):
    ctx, ex = lax.axis_index("ctx"), lax.axis_index("exp")
    query_pos = (ctx * 16 + ex) * tokens + lax.broadcasted_iota(jnp.int32, (tokens, 1), 0)
    begin = jnp.zeros_like(query_pos)
    bound = jnp.int32(0)
    for r in range(lengths.shape[1]):
        bound = bound + lengths[0, r]
        begin = jnp.where(query_pos >= bound, bound, begin)
    first = (ctx * 16 + (ex // 2) * 2 - 16) * tokens
    step = 256
    for c in range(bias.shape[1] // step):
        key_pos = first + c * step + lax.broadcasted_iota(jnp.int32, (tokens, step), 1)
        seen = (key_pos <= query_pos) & (key_pos >= begin)
        bias[:, c * step:(c + 1) * step] = jnp.where(seen, 0.0, -1e30)


def attend(i, queries, window, bias, out):
    tokens, keys = bias.shape
    columns = HEADS_AT_ONCE * HEAD_WIDTH
    place_of = pl.multiple_of(i * columns, columns)
    group = i // (QUERY_HEADS // KEY_HEADS // HEADS_AT_ONCE)
    key_col = pl.multiple_of(group * HEAD_WIDTH, HEAD_WIDTH)
    value_col = pl.multiple_of((KEY_HEADS + group) * HEAD_WIDTH, HEAD_WIDTH)
    key_rows = window[:, :, :, pl.ds(key_col, HEAD_WIDTH)].reshape(keys, HEAD_WIDTH)
    value_rows = window[:, :, :, pl.ds(value_col, HEAD_WIDTH)].reshape(keys, HEAD_WIDTH)
    block = queries[:, pl.ds(place_of, columns)]
    stacked = jnp.concatenate(
        [block[:, h * HEAD_WIDTH:(h + 1) * HEAD_WIDTH] for h in range(HEADS_AT_ONCE)], axis=0
    )
    scores = lax.dot_general(stacked, key_rows, TURNED, preferred_element_type=jnp.float32)
    scores = scores.reshape(HEADS_AT_ONCE, tokens, keys) + bias[...][None]
    top = jnp.max(scores, axis=-1, keepdims=True)
    probs = jnp.exp2((scores - top) * (math.log2(math.e) / math.sqrt(HEAD_WIDTH)))
    total = jnp.sum(probs, axis=-1, keepdims=True)
    summed = jnp.dot(
        probs.reshape(HEADS_AT_ONCE * tokens, keys).astype(jnp.bfloat16), value_rows,
        preferred_element_type=jnp.float32,
    ).reshape(HEADS_AT_ONCE, tokens, HEAD_WIDTH)
    result = (summed / total).astype(out.dtype)
    out[:, pl.ds(place_of, columns)] = jnp.concatenate([result[h] for h in range(HEADS_AT_ONCE)], axis=1)


def kernel(
    w_gate, w_up, w_down, queries, keys, values, hidden, gain, routes, gates, lengths,
    context, mixture,
    wall, window, hidden_rows, query_rows, context_rows, mixture_rows, packed, arrived, results, returned, sums, active, bias,
    local_sem, pass_out, own_in, out_sem, in_sem, share_in, route_out, route_in, kv_out, kv_in, back_out, back_in,
):
    x, y, z, core = place()
    dp, ctx, ex = lax.axis_index("dp"), lax.axis_index("ctx"), lax.axis_index("exp")
    group, partner = x // 2, SIDE - 1 - x
    native = core == group
    beside = x + 1 - 2 * (x % 2)
    above, below, over = lax.rem(y + 1, SIDE), lax.rem(y + SIDE - 1, SIDE), lax.rem(y + 2, SIDE)
    to_beside, to_above, to_below = device_at(beside, y, ex), device_at(x, above, ex), device_at(x, below, ex)
    sibling = z * 2 + 1 - core
    to_sibling = (dp, ctx, sibling)
    prior_ctx, next_ctx = lax.rem(ctx + 7, 8), lax.rem(ctx + 1, 8)
    to_next = (dp, lax.rem(ctx + (z + 1) // DEPTH, 8), lax.rem(ex + 2, 16))
    to_prior = (dp, lax.rem(ctx + 7 + (z + DEPTH - 1) // DEPTH, 8), lax.rem(ex + 14, 16))
    expert = z * 2 + group
    rows_x = jnp.where(native, x, partner)
    quarter = wall.shape[-1]
    count = arrived.shape[1] * arrived.shape[2]

    def at(chip_x, chip_y):
        return chip_y * SIDE + jnp.where(native, chip_x, SIDE - 1 - chip_x)

    def shard_copies(remote):
        copies = []
        for m, source in enumerate((w_gate, w_up, w_down)):
            for q in range(QUARTERS):
                part = source.at[:, pl.ds(q * quarter, quarter)]
                home, arrival = wall.at[m, q, y * SIDE + x], own_in.at[m]
                if remote:
                    copies.append(pltpu.make_async_remote_copy(
                        src_ref=part, dst_ref=home, send_sem=pass_out, recv_sem=arrival,
                        device_id=device_at(partner, y, sibling), device_id_type=MESH,
                    ))
                else:
                    copies.append(pltpu.make_async_copy(part, home, arrival))
        return copies

    @pl.when(native)
    def _():
        for copy in shard_copies(False):
            copy.start()

    width = keys.shape[1]
    key_copy = pltpu.make_async_copy(keys, window.at[DEPTH, core, :, pl.ds(0, width)], local_sem.at[0])
    value_copy = pltpu.make_async_copy(values, window.at[DEPTH, core, :, pl.ds(width, width)], local_sem.at[1])
    hidden_copy = pltpu.make_async_copy(hidden, hidden_rows, local_sem.at[2])
    query_copy = pltpu.make_async_copy(queries, query_rows, local_sem.at[3])
    for copy in (hidden_copy, key_copy, value_copy, query_copy):
        copy.start()

    barrier = pltpu.get_barrier_semaphore()
    for neighbour in (to_beside, to_above, to_below, (dp, prior_ctx, ex), to_next, to_prior):
        pl.semaphore_signal(barrier, inc=1, device_id=neighbour, device_id_type=MESH)
    for step in range(16):
        other = lax.rem(ex + step, 16)
        if step:
            pl.semaphore_signal(barrier, inc=1, device_id=(dp, ctx, other), device_id_type=MESH)
        pl.semaphore_signal(barrier, inc=1, device_id=device_at(partner, y, other), device_id_type=MESH)

    hidden_copy.wait()
    picks = slot_hits(routes[...]).reshape(count, -1).astype(jnp.bfloat16)
    rows = hidden_rows[...].astype(jnp.float32)
    scale = lax.rsqrt(jnp.mean(rows * rows, axis=-1, keepdims=True) + 1e-06)
    for q in range(QUARTERS):
        cols = pl.ds(q * quarter, quarter)
        normed = (hidden_rows[:, cols].astype(jnp.float32) * scale * gain[:, cols]).astype(jnp.bfloat16)
        block = jnp.dot(picks, normed, preferred_element_type=jnp.float32).astype(jnp.bfloat16)
        packed[q] = block.reshape(16, CAP, quarter)
    key_copy.wait()
    value_copy.wait()
    pl.semaphore_wait(barrier, 6 + 15 + 16)

    @pl.when(jnp.logical_not(native))
    def _():
        for copy in shard_copies(True):
            copy.start()

    def send(m, first, number, shard, target, arrival):
        part = wall.at[m, pl.ds(first, number), shard]
        pltpu.make_async_remote_copy(
            src_ref=part, dst_ref=part, send_sem=out_sem.at[m], recv_sem=arrival,
            device_id=target, device_id_type=MESH,
        ).start()

    def landed(m, first, number, shard, index):
        part = wall.at[m, pl.ds(first, number), shard]
        pltpu.make_async_copy(part, part, in_sem.at[m, index]).wait()

    def wait_for(part, semaphore):
        pltpu.make_async_copy(part, part, semaphore).wait()

    def share_shard(m, shard):
        send(m, 0, 4, shard, to_sibling, share_in.at[m])

    def first_round(m):
        wait_for(wall.at[m, :, at(x, y)], own_in.at[m])
        for i, target in enumerate((to_beside, to_above, to_below)):
            send(m, 0, 4, at(x, y), target, in_sem.at[m, i])
        share_shard(m, at(x, y))

    def second_round(m):
        landed(m, 0, 4, at(beside, y), 0)
        send(m, 1, 2, at(beside, y), to_above, in_sem.at[m, 5])
        send(m, 1, 2, at(beside, y), to_below, in_sem.at[m, 8])
        landed(m, 0, 4, at(x, below), 1)
        send(m, 0, 2, at(x, below), to_above, in_sem.at[m, 3])
        send(m, 0, 1, at(x, below), to_beside, in_sem.at[m, 6])
        send(m, 3, 1, at(x, below), to_beside, in_sem.at[m, 7])
        landed(m, 0, 4, at(x, above), 2)
        send(m, 2, 2, at(x, above), to_below, in_sem.at[m, 4])
        send(m, 0, 1, at(x, above), to_beside, in_sem.at[m, 9])
        send(m, 3, 1, at(x, above), to_beside, in_sem.at[m, 10])
        for shard in (at(beside, y), at(x, below), at(x, above)):
            share_shard(m, shard)

    def third_round(m):
        landed(m, 0, 2, at(x, over), 3)
        send(m, 0, 1, at(x, over), to_beside, in_sem.at[m, 11])
        landed(m, 2, 2, at(x, over), 4)
        send(m, 3, 1, at(x, over), to_beside, in_sem.at[m, 14])
        landed(m, 1, 2, at(beside, below), 5)
        send(m, 1, 1, at(beside, below), to_above, in_sem.at[m, 12])
        landed(m, 1, 2, at(beside, above), 8)
        send(m, 2, 1, at(beside, above), to_below, in_sem.at[m, 13])
        share_shard(m, at(x, over))
        for side, index in ((below, 6), (above, 9)):
            landed(m, 0, 1, at(beside, side), index)
            landed(m, 3, 1, at(beside, side), index + 1)
            share_shard(m, at(beside, side))

    def fourth_round(m):
        for q in range(QUARTERS):
            landed(m, q, 1, at(beside, over), 11 + q)
        share_shard(m, at(beside, over))

    def last_round(m):
        wait_for(wall.at[m, :, pl.ds(0, 2 * SIDE)], share_in.at[m])

    def matrix(m, q):
        return wall[m, q].reshape(-1, quarter)

    def project(m):
        @pl.loop(0, QUARTERS)
        def _(q):
            part = lax.dot_general(
                arrived[q].reshape(count, quarter), matrix(m, q), TURNED, preferred_element_type=jnp.float32
            )
            sums[m] = jnp.where(q == 0, part, sums[m] + part)

    def route_copy(q, step, c):
        plane = lax.rem(z + step, DEPTH)
        wanted = plane * 2 + (group if c == 0 else 1 - group)
        return pltpu.make_async_remote_copy(
            src_ref=packed.at[q, wanted], dst_ref=arrived.at[q, ex],
            send_sem=route_out.at[q], recv_sem=route_in.at[q],
            device_id=device_at(x if c == 0 else partner, y, plane * 2 + group), device_id_type=MESH,
        )

    def back_copy(q, step, c):
        source = lax.rem(z + step, DEPTH) * 2 + (core if c == 0 else 1 - core)
        return pltpu.make_async_remote_copy(
            src_ref=results.at[q, source], dst_ref=returned.at[q, expert],
            send_sem=back_out.at[q], recv_sem=back_in.at[q],
            device_id=device_at(rows_x, y, source), device_id_type=MESH,
        )

    far_first = (4, 3, 5, 2, 6, 1, 7, 0)

    def scatter(make, q, own):
        for step in far_first:
            for c in (0, 1):
                if step or c:
                    make(q, step, c).start()

        @pl.when(native)
        def _():
            own.start()

        @pl.when(jnp.logical_not(native))
        def _():
            make(q, 0, 0).start()

    def scattered(block, semaphore):
        @pl.when(native)
        def _():
            wait_for(block.at[pl.ds(0, 15)], semaphore)

        @pl.when(jnp.logical_not(native))
        def _():
            wait_for(block, semaphore)

    def send_rows(q):
        scatter(route_copy, q, pltpu.make_async_copy(packed.at[q, ex], arrived.at[q, ex], route_in.at[q]))

    def pass_block(source, target, device, arrival):
        pltpu.make_async_remote_copy(
            src_ref=window.at[source, core], dst_ref=window.at[target, core],
            send_sem=kv_out.at[0], recv_sem=kv_in.at[arrival],
            device_id=device, device_id_type=MESH,
        ).start()

    def pass_blocks(hop):
        if hop == 1:
            wait_for(window.at[0, core], kv_in.at[0])
        else:
            wait_for(window.at[DEPTH + 1 - hop, core], kv_in.at[2 * hop - 3])
            wait_for(window.at[hop - 1, core], kv_in.at[2 * hop - 2])
        if hop < DEPTH // 2:
            pass_block(DEPTH + 1 - hop, DEPTH - hop, to_next, 2 * hop - 1)
            pass_block(hop - 1, hop, to_prior, 2 * hop)
        else:
            onwards = core == 0
            device = tuple(jnp.where(onwards, a, b) for a, b in zip(to_next, to_prior))
            pass_block(jnp.where(onwards, DEPTH // 2 + 1, DEPTH // 2 - 1), DEPTH // 2, device, DEPTH - 1)

    send_rows(0)

    @pl.when(native)
    def _():
        first_round(0)
        first_round(1)

    pass_block(DEPTH, 0, (dp, next_ctx, ex), 0)
    for q in range(1, QUARTERS):
        send_rows(q)

    @pl.when(jnp.logical_not(native))
    def _():
        first_round(0)
        first_round(1)

    second_round(0)
    first_round(2)
    second_round(1)
    third_round(0)
    second_round(2)
    third_round(1)
    fourth_round(0)
    pass_blocks(1)
    third_round(2)
    fourth_round(1)
    last_round(0)
    pass_blocks(2)
    for q in range(QUARTERS):
        wait_for(arrived.at[q], route_in.at[q])
    project(0)
    fourth_round(2)
    pass_blocks(3)
    last_round(1)
    project(1)
    g = sums[0]
    active[...] = (g / (1.0 + jnp.exp(-g)) * sums[1]).astype(jnp.bfloat16)
    pass_blocks(4)
    last_round(2)

    for q in range(QUARTERS):
        block = jnp.dot(active[...], matrix(2, q), preferred_element_type=jnp.float32)
        results[q] = block.astype(jnp.bfloat16).reshape(16, CAP, quarter)
        scatter(back_copy, q, pltpu.make_async_copy(results.at[q, ex], returned.at[q, ex], back_in.at[q]))

    wait_for(window.at[DEPTH // 2, core], kv_in.at[DEPTH - 1])
    share = pltpu.make_async_remote_copy(
        src_ref=window.at[:, core], dst_ref=window.at[:, core],
        send_sem=kv_out.at[1], recv_sem=kv_in.at[DEPTH],
        device_id=to_sibling, device_id_type=MESH,
    )
    share.start()
    attention_bias(lengths, query_rows.shape[0], bias)
    query_copy.wait()
    wait_for(window.at[:, 1 - core], kv_in.at[DEPTH])

    @pl.loop(0, QUERY_HEADS // HEADS_AT_ONCE)
    def _(i):
        attend(i, query_rows, window, bias, context_rows)

    context_copy = pltpu.make_async_copy(context_rows, context, local_sem.at[4])
    context_copy.start()
    ids = lax.broadcasted_iota(jnp.int32, (16, routes.shape[1]), 0)
    weight = jnp.where(ids == routes[0:1, :], gates[0:1, :], 0.0)
    weight = weight + jnp.where(ids == routes[1:2, :], gates[1:2, :], 0.0)
    spread = (slot_hits(routes[...]) * weight[:, None, :]).reshape(count, -1)
    high = spread.astype(jnp.bfloat16)
    low = (spread - high.astype(jnp.float32)).astype(jnp.bfloat16)
    by_slot = (((0,), (0,)), ((), ()))
    mixture_copies = []
    for q in range(QUARTERS):
        wait_for(returned.at[q], back_in.at[q])
        block = returned[q].reshape(count, quarter)
        total = lax.dot_general(high, block, by_slot, preferred_element_type=jnp.float32)
        total = total + lax.dot_general(low, block, by_slot, preferred_element_type=jnp.float32)
        cols = pl.ds(q * quarter, quarter)
        mixture_rows[:, cols] = total.astype(mixture.dtype)
        copy = pltpu.make_async_copy(mixture_rows.at[:, cols], mixture.at[:, cols], local_sem.at[5 + q])
        copy.start()
        mixture_copies.append(copy)

    share.wait_send()
    wait_for(window.at[pl.ds(0, DEPTH), core], kv_out.at[0])
    for m in range(3):
        wait_for(wall.at[m, :, pl.ds(0, 15)], out_sem.at[m])
    for q in range(QUARTERS):
        scattered(packed.at[q], route_out.at[q])
        scattered(results.at[q], back_out.at[q])

    @pl.when(jnp.logical_not(native))
    def _():
        wait_for(wall.at[:, :, y * SIDE + x], pass_out)

    context_copy.wait()
    for copy in mixture_copies:
        copy.wait()


def shards(queries, keys, values, lengths, hidden, norm_gain, routes, gates, w_gate, w_up, w_down):
    tokens, width = hidden.shape
    turned = [jnp.swapaxes(w[0], 0, 1) for w in (w_gate, w_up, w_down)]
    piece, quarter = turned[0].shape[0], width // QUARTERS
    units, count = piece * SIDE * SIDE, 16 * CAP
    far, vmem = pl.BlockSpec(memory_space=pltpu.HBM), pl.BlockSpec(memory_space=pltpu.VMEM)
    bf16, f32, dma = jnp.bfloat16, jnp.float32, pltpu.SemaphoreType.DMA
    out = jax.ShapeDtypeStruct((tokens, width), bf16)
    return pl.pallas_call(
        kernel,
        out_shape=(out, out),
        in_specs=[far] * 7 + [vmem] * 3 + [pl.BlockSpec(memory_space=pltpu.SMEM)],
        out_specs=[far] * 2,
        scratch_shapes=[
            pltpu.VMEM((3, QUARTERS, SIDE * SIDE, piece, quarter), bf16),
            pltpu.VMEM((DEPTH + 1, 2, tokens, 2 * keys.shape[1]), bf16),
            pltpu.VMEM((tokens, width), bf16),
            pltpu.VMEM((tokens, width), bf16),
            pltpu.VMEM((tokens, width), bf16),
            pltpu.VMEM((tokens, width), bf16),
            pltpu.VMEM((QUARTERS, 16, CAP, quarter), bf16),
            pltpu.VMEM((QUARTERS, 16, CAP, quarter), bf16),
            pltpu.VMEM((QUARTERS, 16, CAP, quarter), bf16),
            pltpu.VMEM((QUARTERS, 16, CAP, quarter), bf16),
            pltpu.VMEM((2, count, units), f32),
            pltpu.VMEM((count, units), bf16),
            pltpu.VMEM((tokens, (DEPTH + 1) * 2 * tokens), f32),
            dma((9,)), dma(()), dma((3,)), dma((3,)), dma((3, 15)), dma((3,)), dma((QUARTERS,)), dma((QUARTERS,)),
            dma((2,)), dma((DEPTH + 1,)), dma((QUARTERS,)), dma((QUARTERS,)),
        ],
        compiler_params=pltpu.CompilerParams(
            collective_id=0, has_side_effects=True, vmem_limit_bytes=60 * 1024 * 1024
        ),
        cost_estimate=pl.CostEstimate(flops=20 * 10**9, bytes_accessed=10 * 10**6, transcendentals=10**7),
        name="whole_block",
    )(*turned, queries, keys, values, hidden, norm_gain[None, :], routes.T, gates.T, lengths)


def solution(mesh):
    whole = P(("dp", "ctx", "exp"), None)
    weights = P("exp", None, ("dp", "ctx"))
    return jax.shard_map(
        shards,
        mesh=mesh,
        in_specs=(whole, whole, whole, P("dp", None), whole, P(), whole, whole, weights, weights, weights),
        out_specs=(whole, whole),
        check_vma=False,
    )
```

```python
import math

import jax
import jax.numpy as jnp
from jax import lax
from jax.experimental import pallas as pl
from jax.experimental.pallas import tpu as pltpu
from jax.sharding import PartitionSpec as P

MESH = pl.DeviceIdType.MESH
HEAD_WIDTH = 128
QUERY_HEADS = 32
KEY_HEADS = 2
SIDE = 4
DEPTH = 8
QUARTERS = 4
CAP = 24
HEADS_AT_ONCE = 4
TURNED = (((1,), (1,)), ((), ()))


def place():
    dp, ctx, ex = lax.axis_index("dp"), lax.axis_index("ctx"), lax.axis_index("exp")
    return (ctx % 2) * 2 + dp, ctx // 2, ex // 2, ex % 2


def device_at(x, y, ex):
    return (x % 2, y * 2 + x // 2, ex)


def slot_hits(routes):
    experts, tokens = 16, routes.shape[1]
    ids = lax.broadcasted_iota(jnp.int32, (experts, tokens), 0)
    hits = ((ids == routes[0:1, :]) | (ids == routes[1:2, :])).astype(jnp.float32)
    earlier = (
        lax.broadcasted_iota(jnp.int32, (tokens, tokens), 0)
        < lax.broadcasted_iota(jnp.int32, (tokens, tokens), 1)
    ).astype(jnp.bfloat16)
    ranks = jnp.dot(hits.astype(jnp.bfloat16), earlier, preferred_element_type=jnp.float32)
    ranks = jnp.where(hits > 0, ranks, -1.0).astype(jnp.int32)
    wanted = lax.broadcasted_iota(jnp.int32, (experts, CAP, tokens), 1)
    return (ranks[:, None, :] == wanted).astype(jnp.float32)


def attention_bias(lengths, tokens, bias):
    ctx, ex = lax.axis_index("ctx"), lax.axis_index("exp")
    query_pos = (ctx * 16 + ex) * tokens + lax.broadcasted_iota(jnp.int32, (tokens, 1), 0)
    begin = jnp.zeros_like(query_pos)
    bound = jnp.int32(0)
    for r in range(lengths.shape[1]):
        bound = bound + lengths[0, r]
        begin = jnp.where(query_pos >= bound, bound, begin)
    first = (ctx * 16 + (ex // 2) * 2 - 16) * tokens
    step = 256
    for c in range(bias.shape[1] // step):
        key_pos = first + c * step + lax.broadcasted_iota(jnp.int32, (tokens, step), 1)
        seen = (key_pos <= query_pos) & (key_pos >= begin)
        bias[:, c * step:(c + 1) * step] = jnp.where(seen, 0.0, -1e30)


def attend(i, queries, window, bias, out):
    tokens, keys = bias.shape
    columns = HEADS_AT_ONCE * HEAD_WIDTH
    place_of = pl.multiple_of(i * columns, columns)
    group = i // (QUERY_HEADS // KEY_HEADS // HEADS_AT_ONCE)
    key_col = pl.multiple_of(group * HEAD_WIDTH, HEAD_WIDTH)
    value_col = pl.multiple_of((KEY_HEADS + group) * HEAD_WIDTH, HEAD_WIDTH)
    key_rows = window[:, :, :, pl.ds(key_col, HEAD_WIDTH)].reshape(keys, HEAD_WIDTH)
    value_rows = window[:, :, :, pl.ds(value_col, HEAD_WIDTH)].reshape(keys, HEAD_WIDTH)
    block = queries[:, pl.ds(place_of, columns)]
    stacked = jnp.concatenate(
        [block[:, h * HEAD_WIDTH:(h + 1) * HEAD_WIDTH] for h in range(HEADS_AT_ONCE)], axis=0
    )
    scores = lax.dot_general(stacked, key_rows, TURNED, preferred_element_type=jnp.float32)
    scores = scores.reshape(HEADS_AT_ONCE, tokens, keys) + bias[...][None]
    top = jnp.max(scores, axis=-1, keepdims=True)
    probs = jnp.exp2((scores - top) * (math.log2(math.e) / math.sqrt(HEAD_WIDTH)))
    total = jnp.sum(probs, axis=-1, keepdims=True)
    summed = jnp.dot(
        probs.reshape(HEADS_AT_ONCE * tokens, keys).astype(jnp.bfloat16), value_rows,
        preferred_element_type=jnp.float32,
    ).reshape(HEADS_AT_ONCE, tokens, HEAD_WIDTH)
    result = (summed / total).astype(out.dtype)
    out[:, pl.ds(place_of, columns)] = jnp.concatenate([result[h] for h in range(HEADS_AT_ONCE)], axis=1)


def kernel(
    w_gate, w_up, w_down, queries, keys, values, hidden, gain, routes, gates, lengths,
    context, mixture,
    wall, window, hidden_rows, query_rows, context_rows, mixture_rows, packed, arrived, results, returned, sums, active, bias,
    local_sem, pass_out, own_in, out_sem, in_sem, share_in, route_out, route_in, kv_out, kv_in, back_out, back_in,
):
    x, y, z, core = place()
    dp, ctx, ex = lax.axis_index("dp"), lax.axis_index("ctx"), lax.axis_index("exp")
    group, partner = x // 2, SIDE - 1 - x
    native = core == group
    beside = x + 1 - 2 * (x % 2)
    above, below, over = lax.rem(y + 1, SIDE), lax.rem(y + SIDE - 1, SIDE), lax.rem(y + 2, SIDE)
    to_beside, to_above, to_below = device_at(beside, y, ex), device_at(x, above, ex), device_at(x, below, ex)
    sibling = z * 2 + 1 - core
    to_sibling = (dp, ctx, sibling)
    prior_ctx, next_ctx = lax.rem(ctx + 7, 8), lax.rem(ctx + 1, 8)
    to_next = (dp, lax.rem(ctx + (z + 1) // DEPTH, 8), lax.rem(ex + 2, 16))
    to_prior = (dp, lax.rem(ctx + 7 + (z + DEPTH - 1) // DEPTH, 8), lax.rem(ex + 14, 16))
    expert = z * 2 + group
    rows_x = jnp.where(native, x, partner)
    quarter = wall.shape[-1]
    count = arrived.shape[1] * arrived.shape[2]

    def at(chip_x, chip_y):
        return chip_y * SIDE + jnp.where(native, chip_x, SIDE - 1 - chip_x)

    def shard_copies(remote):
        copies = []
        for m, source in enumerate((w_gate, w_up, w_down)):
            for q in range(QUARTERS):
                part = source.at[:, pl.ds(q * quarter, quarter)]
                home, arrival = wall.at[m, q, y * SIDE + x], own_in.at[m]
                if remote:
                    copies.append(pltpu.make_async_remote_copy(
                        src_ref=part, dst_ref=home, send_sem=pass_out, recv_sem=arrival,
                        device_id=device_at(partner, y, sibling), device_id_type=MESH,
                    ))
                else:
                    copies.append(pltpu.make_async_copy(part, home, arrival))
        return copies

    @pl.when(native)
    def _():
        for copy in shard_copies(False):
            copy.start()

    width = keys.shape[1]
    key_copy = pltpu.make_async_copy(keys, window.at[DEPTH, core, :, pl.ds(0, width)], local_sem.at[0])
    value_copy = pltpu.make_async_copy(values, window.at[DEPTH, core, :, pl.ds(width, width)], local_sem.at[1])
    hidden_copy = pltpu.make_async_copy(hidden, hidden_rows, local_sem.at[2])
    query_copy = pltpu.make_async_copy(queries, query_rows, local_sem.at[3])
    for copy in (hidden_copy, key_copy, value_copy, query_copy):
        copy.start()

    barrier = pltpu.get_barrier_semaphore()
    for neighbour in (to_beside, to_above, to_below, (dp, prior_ctx, ex), to_next, to_prior):
        pl.semaphore_signal(barrier, inc=1, device_id=neighbour, device_id_type=MESH)
    for step in range(16):
        other = lax.rem(ex + step, 16)
        if step:
            pl.semaphore_signal(barrier, inc=1, device_id=(dp, ctx, other), device_id_type=MESH)
        pl.semaphore_signal(barrier, inc=1, device_id=device_at(partner, y, other), device_id_type=MESH)

    hidden_copy.wait()
    picks = slot_hits(routes[...]).reshape(count, -1).astype(jnp.bfloat16)
    rows = hidden_rows[...].astype(jnp.float32)
    scale = lax.rsqrt(jnp.mean(rows * rows, axis=-1, keepdims=True) + 1e-06)
    for q in range(QUARTERS):
        cols = pl.ds(q * quarter, quarter)
        normed = (hidden_rows[:, cols].astype(jnp.float32) * scale * gain[:, cols]).astype(jnp.bfloat16)
        block = jnp.dot(picks, normed, preferred_element_type=jnp.float32).astype(jnp.bfloat16)
        packed[q] = block.reshape(16, CAP, quarter)
    key_copy.wait()
    value_copy.wait()
    pl.semaphore_wait(barrier, 6 + 15 + 16)

    @pl.when(jnp.logical_not(native))
    def _():
        for copy in shard_copies(True):
            copy.start()

    def send(m, first, number, shard, target, arrival):
        part = wall.at[m, pl.ds(first, number), shard]
        pltpu.make_async_remote_copy(
            src_ref=part, dst_ref=part, send_sem=out_sem.at[m], recv_sem=arrival,
            device_id=target, device_id_type=MESH,
        ).start()

    def landed(m, first, number, shard, index):
        part = wall.at[m, pl.ds(first, number), shard]
        pltpu.make_async_copy(part, part, in_sem.at[m, index]).wait()

    def wait_for(part, semaphore):
        pltpu.make_async_copy(part, part, semaphore).wait()

    def share_shard(m, shard):
        send(m, 0, 4, shard, to_sibling, share_in.at[m])

    def first_round(m):
        wait_for(wall.at[m, :, at(x, y)], own_in.at[m])
        for i, target in enumerate((to_beside, to_above, to_below)):
            send(m, 0, 4, at(x, y), target, in_sem.at[m, i])
        share_shard(m, at(x, y))

    def second_round(m):
        landed(m, 0, 4, at(beside, y), 0)
        send(m, 1, 2, at(beside, y), to_above, in_sem.at[m, 5])
        send(m, 1, 2, at(beside, y), to_below, in_sem.at[m, 8])
        landed(m, 0, 4, at(x, below), 1)
        send(m, 0, 2, at(x, below), to_above, in_sem.at[m, 3])
        send(m, 0, 1, at(x, below), to_beside, in_sem.at[m, 6])
        send(m, 3, 1, at(x, below), to_beside, in_sem.at[m, 7])
        landed(m, 0, 4, at(x, above), 2)
        send(m, 2, 2, at(x, above), to_below, in_sem.at[m, 4])
        send(m, 0, 1, at(x, above), to_beside, in_sem.at[m, 9])
        send(m, 3, 1, at(x, above), to_beside, in_sem.at[m, 10])
        for shard in (at(beside, y), at(x, below), at(x, above)):
            share_shard(m, shard)

    def third_round(m):
        landed(m, 0, 2, at(x, over), 3)
        send(m, 0, 1, at(x, over), to_beside, in_sem.at[m, 11])
        landed(m, 2, 2, at(x, over), 4)
        send(m, 3, 1, at(x, over), to_beside, in_sem.at[m, 14])
        landed(m, 1, 2, at(beside, below), 5)
        send(m, 1, 1, at(beside, below), to_above, in_sem.at[m, 12])
        landed(m, 1, 2, at(beside, above), 8)
        send(m, 2, 1, at(beside, above), to_below, in_sem.at[m, 13])
        share_shard(m, at(x, over))
        for side, index in ((below, 6), (above, 9)):
            landed(m, 0, 1, at(beside, side), index)
            landed(m, 3, 1, at(beside, side), index + 1)
            share_shard(m, at(beside, side))

    def fourth_round(m):
        for q in range(QUARTERS):
            landed(m, q, 1, at(beside, over), 11 + q)
        share_shard(m, at(beside, over))

    def last_round(m):
        wait_for(wall.at[m, :, pl.ds(0, 2 * SIDE)], share_in.at[m])

    def matrix(m, q):
        return wall[m, q].reshape(-1, quarter)

    def project(m):
        @pl.loop(0, QUARTERS)
        def _(q):
            part = lax.dot_general(
                arrived[q].reshape(count, quarter), matrix(m, q), TURNED, preferred_element_type=jnp.float32
            )
            sums[m] = jnp.where(q == 0, part, sums[m] + part)

    def route_copy(q, step, c):
        plane = lax.rem(z + step, DEPTH)
        wanted = plane * 2 + (group if c == 0 else 1 - group)
        return pltpu.make_async_remote_copy(
            src_ref=packed.at[q, wanted], dst_ref=arrived.at[q, ex],
            send_sem=route_out.at[q], recv_sem=route_in.at[q],
            device_id=device_at(x if c == 0 else partner, y, plane * 2 + group), device_id_type=MESH,
        )

    def back_copy(q, step, c):
        source = lax.rem(z + step, DEPTH) * 2 + (core if c == 0 else 1 - core)
        return pltpu.make_async_remote_copy(
            src_ref=results.at[q, source], dst_ref=returned.at[q, expert],
            send_sem=back_out.at[q], recv_sem=back_in.at[q],
            device_id=device_at(rows_x, y, source), device_id_type=MESH,
        )

    far_first = (4, 3, 5, 2, 6, 1, 7, 0)

    def scatter(make, q, own):
        for step in far_first:
            for c in (0, 1):
                if step or c:
                    make(q, step, c).start()

        @pl.when(native)
        def _():
            own.start()

        @pl.when(jnp.logical_not(native))
        def _():
            make(q, 0, 0).start()

    def scattered(block, semaphore):
        @pl.when(native)
        def _():
            wait_for(block.at[pl.ds(0, 15)], semaphore)

        @pl.when(jnp.logical_not(native))
        def _():
            wait_for(block, semaphore)

    def send_rows(q):
        scatter(route_copy, q, pltpu.make_async_copy(packed.at[q, ex], arrived.at[q, ex], route_in.at[q]))

    def wait_rows(q):
        scattered(packed.at[q], route_out.at[q])

    def pass_block(source, target, device, arrival):
        rows = window.shape[2] // 8
        for part in range(8):
            block = pl.ds(part * rows, rows)
            pltpu.make_async_remote_copy(
                src_ref=window.at[source, core, block], dst_ref=window.at[target, core, block],
                send_sem=kv_out.at[0], recv_sem=kv_in.at[arrival],
                device_id=device, device_id_type=MESH,
            ).start()

    def pass_blocks(hop):
        if hop == 1:
            wait_for(window.at[0, core], kv_in.at[0])
        else:
            wait_for(window.at[DEPTH + 1 - hop, core], kv_in.at[2 * hop - 3])
            wait_for(window.at[hop - 1, core], kv_in.at[2 * hop - 2])
        if hop < DEPTH // 2:
            pass_block(DEPTH + 1 - hop, DEPTH - hop, to_next, 2 * hop - 1)
            pass_block(hop - 1, hop, to_prior, 2 * hop)
        else:
            onwards = core == 0
            device = tuple(jnp.where(onwards, a, b) for a, b in zip(to_next, to_prior))
            pass_block(jnp.where(onwards, DEPTH // 2 + 1, DEPTH // 2 - 1), DEPTH // 2, device, DEPTH - 1)

    send_rows(0)

    @pl.when(native)
    def _():
        first_round(0)
        first_round(1)

    pass_block(DEPTH, 0, (dp, next_ctx, ex), 0)
    send_rows(1)
    send_rows(2)

    @pl.when(jnp.logical_not(native))
    def _():
        first_round(0)
        first_round(1)

    second_round(0)
    first_round(2)
    second_round(1)
    pass_blocks(1)
    third_round(0)
    second_round(2)
    third_round(1)
    wait_rows(0)
    send_rows(3)
    fourth_round(0)
    third_round(2)
    fourth_round(1)
    pass_blocks(2)
    last_round(0)
    for q in range(QUARTERS):
        wait_for(arrived.at[q], route_in.at[q])
    pass_blocks(3)
    project(0)
    fourth_round(2)
    last_round(1)
    project(1)
    g = sums[0]
    active[...] = (g / (1.0 + jnp.exp(-g)) * sums[1]).astype(jnp.bfloat16)
    pass_blocks(4)
    last_round(2)

    for q in range(QUARTERS):
        block = jnp.dot(active[...], matrix(2, q), preferred_element_type=jnp.float32)
        results[q] = block.astype(jnp.bfloat16).reshape(16, CAP, quarter)
        scatter(back_copy, q, pltpu.make_async_copy(results.at[q, ex], returned.at[q, ex], back_in.at[q]))

    wait_for(window.at[DEPTH // 2, core], kv_in.at[DEPTH - 1])
    share = pltpu.make_async_remote_copy(
        src_ref=window.at[:, core], dst_ref=window.at[:, core],
        send_sem=kv_out.at[1], recv_sem=kv_in.at[DEPTH],
        device_id=to_sibling, device_id_type=MESH,
    )
    share.start()
    attention_bias(lengths, query_rows.shape[0], bias)
    query_copy.wait()
    wait_for(window.at[:, 1 - core], kv_in.at[DEPTH])

    @pl.loop(0, QUERY_HEADS // HEADS_AT_ONCE)
    def _(i):
        attend(i, query_rows, window, bias, context_rows)

    context_copy = pltpu.make_async_copy(context_rows, context, local_sem.at[4])
    context_copy.start()
    ids = lax.broadcasted_iota(jnp.int32, (16, routes.shape[1]), 0)
    weight = jnp.where(ids == routes[0:1, :], gates[0:1, :], 0.0)
    weight = weight + jnp.where(ids == routes[1:2, :], gates[1:2, :], 0.0)
    spread = (slot_hits(routes[...]) * weight[:, None, :]).reshape(count, -1)
    high = spread.astype(jnp.bfloat16)
    low = (spread - high.astype(jnp.float32)).astype(jnp.bfloat16)
    by_slot = (((0,), (0,)), ((), ()))
    mixture_copies = []
    for q in range(QUARTERS):
        wait_for(returned.at[q], back_in.at[q])
        block = returned[q].reshape(count, quarter)
        total = lax.dot_general(high, block, by_slot, preferred_element_type=jnp.float32)
        total = total + lax.dot_general(low, block, by_slot, preferred_element_type=jnp.float32)
        cols = pl.ds(q * quarter, quarter)
        mixture_rows[:, cols] = total.astype(mixture.dtype)
        copy = pltpu.make_async_copy(mixture_rows.at[:, cols], mixture.at[:, cols], local_sem.at[5 + q])
        copy.start()
        mixture_copies.append(copy)

    share.wait_send()
    wait_for(window.at[pl.ds(0, DEPTH), core], kv_out.at[0])
    for m in range(3):
        wait_for(wall.at[m, :, pl.ds(0, 15)], out_sem.at[m])
    for q in range(QUARTERS):
        if q >= 1:
            scattered(packed.at[q], route_out.at[q])
        scattered(results.at[q], back_out.at[q])

    @pl.when(jnp.logical_not(native))
    def _():
        wait_for(wall.at[:, :, y * SIDE + x], pass_out)

    context_copy.wait()
    for copy in mixture_copies:
        copy.wait()


def shards(queries, keys, values, lengths, hidden, norm_gain, routes, gates, w_gate, w_up, w_down):
    tokens, width = hidden.shape
    turned = [jnp.swapaxes(w[0], 0, 1) for w in (w_gate, w_up, w_down)]
    piece, quarter = turned[0].shape[0], width // QUARTERS
    units, count = piece * SIDE * SIDE, 16 * CAP
    far, vmem = pl.BlockSpec(memory_space=pltpu.HBM), pl.BlockSpec(memory_space=pltpu.VMEM)
    bf16, f32, dma = jnp.bfloat16, jnp.float32, pltpu.SemaphoreType.DMA
    out = jax.ShapeDtypeStruct((tokens, width), bf16)
    return pl.pallas_call(
        kernel,
        out_shape=(out, out),
        in_specs=[far] * 7 + [vmem] * 3 + [pl.BlockSpec(memory_space=pltpu.SMEM)],
        out_specs=[far] * 2,
        scratch_shapes=[
            pltpu.VMEM((3, QUARTERS, SIDE * SIDE, piece, quarter), bf16),
            pltpu.VMEM((DEPTH + 1, 2, tokens, 2 * keys.shape[1]), bf16),
            pltpu.VMEM((tokens, width), bf16),
            pltpu.VMEM((tokens, width), bf16),
            pltpu.VMEM((tokens, width), bf16),
            pltpu.VMEM((tokens, width), bf16),
            pltpu.VMEM((QUARTERS, 16, CAP, quarter), bf16),
            pltpu.VMEM((QUARTERS, 16, CAP, quarter), bf16),
            pltpu.VMEM((QUARTERS, 16, CAP, quarter), bf16),
            pltpu.VMEM((QUARTERS, 16, CAP, quarter), bf16),
            pltpu.VMEM((2, count, units), f32),
            pltpu.VMEM((count, units), bf16),
            pltpu.VMEM((tokens, (DEPTH + 1) * 2 * tokens), f32),
            dma((9,)), dma(()), dma((3,)), dma((3,)), dma((3, 15)), dma((3,)), dma((QUARTERS,)), dma((QUARTERS,)),
            dma((2,)), dma((DEPTH + 1,)), dma((QUARTERS,)), dma((QUARTERS,)),
        ],
        compiler_params=pltpu.CompilerParams(
            collective_id=0, has_side_effects=True, vmem_limit_bytes=60 * 1024 * 1024
        ),
        cost_estimate=pl.CostEstimate(flops=20 * 10**9, bytes_accessed=10 * 10**6, transcendentals=10**7),
        name="whole_block",
    )(*turned, queries, keys, values, hidden, norm_gain[None, :], routes.T, gates.T, lengths)


def solution(mesh):
    whole = P(("dp", "ctx", "exp"), None)
    weights = P("exp", None, ("dp", "ctx"))
    return jax.shard_map(
        shards,
        mesh=mesh,
        in_specs=(whole, whole, whole, P("dp", None), whole, P(), whole, whole, weights, weights, weights),
        out_specs=(whole, whole),
        check_vma=False,
    )
```
